32 devices in a mesh: groups: 2 (over x), ctx: 8 (over z, y), heads: 2 (over core).
Axes of the slice: x: 2, y: 2, z: 4, core: 2. Of those that a mesh axis runs over, the one named last changes fastest.
Arguments:
- query_vectors: bfloat16 [2048, 16, 128], P(('groups', 'ctx'), 'heads'), parts along dimension 0, may hold values from -5.5 to 5.5
- key_vectors: bfloat16 [2048, 4, 128], P(('groups', 'ctx'), 'heads'), parts along dimension 0, may hold values from -5.5 to 5.5
- value_rows: bfloat16 [2048, 4, 128], P(('groups', 'ctx'), 'heads'), parts along dimension 0, may hold values from -6 to 6
- forward_out: bfloat16 [2048, 16, 128], P(('groups', 'ctx'), 'heads'), parts along dimension 0, may hold values from -3 to 3
- out_grad: bfloat16 [2048, 16, 128], P(('groups', 'ctx'), 'heads'), parts along dimension 0, may hold values from -24 to 24
- block_offsets: int32 [16], P(('groups', 'ctx')), parts along dimension 0, may hold values from 0 to 7, each once
Outputs:
- query_grad: float32 [2048, 16, 128], P(('groups', 'ctx'), 'heads'), parts along dimension 0
- key_gradient_array: float32 [2048, 4, 128], P(('groups', 'ctx'), 'heads'), parts along dimension 0
- value_gradient_array: float32 [2048, 4, 128], P(('groups', 'ctx'), 'heads'), parts along dimension 0
The draws below stay inside these ranges and needn't reach their ends.
There are 2 independent parts, one for each index of `groups`. The reference program is written for one: setup_inputs(seed, part) draws one part's arguments, and reference() takes and returns one part's arrays. A program takes and returns all parts, laid end to end along the dimension named above; each array names one. Nothing has to cross between parts.
Inputs may be any that keep to these rules, and one draw needn't show every extreme that they name: block_offsets is a permutation of 0 to 7.
All inputs are finite; a program needn't handle non-finite values.
Results may differ from the reference program's by a relative error of at most 0.0029.
Values may be sent and summed in bfloat16 or wider, within the bound.
A program may use at most 64 MiB of HBM per device.

```python
import jax
import jax.numpy as jnp
from jax import lax

QUERY_HEADS = 16
KEY_VALUE_HEADS = 4
HEAD_SIZE = 128
TOK_DEV = 128
SEQUENCE_TOKENS = 1024
N_CTX = 8


def drawn_keys(key):
    starting_sample = jnp.clip(jax.random.normal(jax.random.fold_in(key, 11), (SEQUENCE_TOKENS, KEY_VALUE_HEADS, HEAD_SIZE), jnp.float32), -5.5, 5.5)
    return starting_sample


def draw_key_vectors(key, part):
    starting_sample = drawn_keys(key)
    result = starting_sample
    return result.astype(jnp.bfloat16)


def draw_query_vectors(key, part):
    starting_sample = jnp.clip(jax.random.normal(jax.random.fold_in(key, 21), (SEQUENCE_TOKENS, QUERY_HEADS, HEAD_SIZE), jnp.float32), -5.5, 5.5)
    result = starting_sample
    return result.astype(jnp.bfloat16)


def level_of(stream_key, extent, split, low, top_value):
    factor_of = 1.0
    for position, parts in split:
        heights = jax.random.uniform(jax.random.fold_in(jax.random.fold_in(stream_key, 6), position), (parts,), jnp.float32, low / len(split), top_value / len(split))
        factor_of = factor_of * jnp.repeat(jnp.exp(heights), extent[position] // parts).reshape((-1,) + (1,) * (len(extent) - 1 - position))
    return factor_of


def noise(rng, dims, width, bound, cuts=(), kind=jnp.bfloat16):
    drawn = jax.random.normal(rng, dims, jnp.float32) * width
    if len(cuts) > 0:
        drawn = level_of(rng, dims, cuts, -0.22, 0.18) * drawn
    return jnp.clip(drawn, min=-bound, max=bound).astype(kind)


def setup_inputs(seed: int = 0, part: int = 0) -> dict:
    seeds = jax.random.split(jax.random.key(seed), 7)
    part_keys = jax.random.split(jax.random.fold_in(seeds[6], part), 7)
    query_vectors = draw_query_vectors(jax.random.fold_in(jax.random.fold_in(seeds[6], part), 71), part)
    key_vectors = draw_key_vectors(jax.random.fold_in(jax.random.fold_in(seeds[6], part), 71), part)
    value_rows = noise(part_keys[2], (SEQUENCE_TOKENS, KEY_VALUE_HEADS, HEAD_SIZE), 1.0, 6.0, ((0, 8), (1, 2)))
    forward_out = noise(part_keys[3], (SEQUENCE_TOKENS, QUERY_HEADS, HEAD_SIZE), 0.5, 3.0, ((0, 8), (1, 2)))
    out_grad = noise(part_keys[4], (SEQUENCE_TOKENS, QUERY_HEADS, HEAD_SIZE), 4.0, 24.0, ((0, 8), (1, 2)))
    block_offsets = jax.random.permutation(part_keys[5], N_CTX).astype(jnp.int32)
    return {"query_vectors": query_vectors, "key_vectors": key_vectors, "value_rows": value_rows, "forward_out": forward_out, "out_grad": out_grad, "block_offsets": block_offsets}


def reference(query_vectors, key_vectors, value_rows, forward_out, out_grad, block_offsets):
    token_index = jnp.arange(SEQUENCE_TOKENS, dtype=jnp.int32)
    positions = block_offsets[token_index // TOK_DEV] * TOK_DEV + token_index % TOK_DEV
    visible = positions[None, :] <= positions[:, None]
    score_scale = HEAD_SIZE ** -0.5
    heads_per_group = QUERY_HEADS // KEY_VALUE_HEADS
    row_delta = jnp.sum(out_grad.astype(jnp.float32) * forward_out.astype(jnp.float32), axis=2)

    def one_head(head):
        kv_head = head // heads_per_group
        q_head = lax.dynamic_index_in_dim(query_vectors, head, 1, keepdims=False)
        g_head = lax.dynamic_index_in_dim(out_grad, head, 1, keepdims=False)
        k_head = lax.dynamic_index_in_dim(key_vectors, kv_head, 1, keepdims=False)
        v_head = lax.dynamic_index_in_dim(value_rows, kv_head, 1, keepdims=False)
        delta_head = lax.dynamic_index_in_dim(row_delta, head, 1, keepdims=False)
        scores = jnp.dot(q_head, k_head.T, preferred_element_type=jnp.float32) * score_scale
        scores = jnp.where(visible, scores, -1e30)
        row_max = jnp.max(scores, axis=1, keepdims=True)
        log_total = row_max + jnp.log(jnp.sum(jnp.exp(scores - row_max), axis=1, keepdims=True))
        probs = jnp.where(visible, jnp.exp(scores - log_total), 0.0)
        probs_low = probs.astype(jnp.bfloat16)
        prob_grad = jnp.dot(g_head, v_head.T, preferred_element_type=jnp.float32)
        score_grad = (probs * (prob_grad - delta_head[:, None])).astype(jnp.bfloat16)
        q_grad = jnp.dot(score_grad, k_head, preferred_element_type=jnp.float32) * score_scale
        k_grad = jnp.dot(score_grad.T, q_head, preferred_element_type=jnp.float32) * score_scale
        v_grad = jnp.dot(probs_low.T, g_head, preferred_element_type=jnp.float32)
        return q_grad, k_grad, v_grad

    q_grads, key_gradients, value_gradients = lax.map(one_head, jnp.arange(QUERY_HEADS, dtype=jnp.int32))
    query_grad = jnp.transpose(q_grads, (1, 0, 2))
    key_gradient_array = jnp.transpose(key_gradients.reshape(KEY_VALUE_HEADS, heads_per_group, SEQUENCE_TOKENS, HEAD_SIZE).sum(axis=1), (1, 0, 2))
    value_gradient_array = jnp.transpose(value_gradients.reshape(KEY_VALUE_HEADS, heads_per_group, SEQUENCE_TOKENS, HEAD_SIZE).sum(axis=1), (1, 0, 2))
    return query_grad, key_gradient_array, value_gradient_array
```

```python
import functools

import jax
import jax.numpy as jnp
from jax import lax
from jax.experimental import pallas as pl
from jax.experimental.pallas import tpu as pltpu
from jax.sharding import PartitionSpec as P

MESH = pl.DeviceIdType.MESH
LOG2E = 1.4426950408889634
F32 = jnp.float32
BF16 = jnp.bfloat16


def dot_nt(a, b):
    return lax.dot_general(a, b, (((1,), (1,)), ((), ())), preferred_element_type=F32)


def dot_nn(a, b):
    return lax.dot_general(a, b, (((1,), (0,)), ((), ())), preferred_element_type=F32)


def kernel(Z, Y, G, H, T, D, *refs):
    (q_ref, k_ref, v_ref, fo_ref, do_ref, off_ref, dq_ref, dk_ref, dv_ref,
     tmp, qs, dos, kbuf, vbuf, kt, s_scr, delta, dqt,
     partv, partk, ysv, ysk, yrv, yrk, zsv, zsk, zrv, zrk,
     kz_s, kz_r, ky_s, ky_r, vz_s, vz_r, vy_s, vy_r,
     gvy_s, gvy_r, gky_s, gky_r, gvz_s, gvz_r, gkz_s, gkz_r) = refs
    me = lax.axis_index("ctx")
    z, y = me // Y, me % Y
    scale = D ** (-0.5)
    N = Z * Y
    R = G * T
    Q = H * T

    def at(zz, yy):
        return {"ctx": zz * Y + yy}

    def up(d):
        return lax.rem(z + d, Z)

    def down(d):
        return lax.rem(z + Z - d, Z)

    other = 1 - y

    barrier = pltpu.get_barrier_semaphore()
    for d in range(1, Z):
        pl.semaphore_signal(barrier, inc=1, device_id=at(up(d), y), device_id_type=MESH)
    if Y == 2:
        pl.semaphore_signal(barrier, inc=1, device_id=at(z, other), device_id_type=MESH)

    def split_heads(src, heads, put):
        tmp[0:T * heads, :] = src[...].astype(F32)
        for h in range(heads):
            put(h, tmp[pl.ds(h, T, stride=heads), :])

    def put_k(g, x):
        kbuf[me, pl.ds(g * T, T), :] = x.astype(BF16)

    def put_v(g, x):
        vbuf[me, pl.ds(g * T, T), :] = x.astype(BF16)

    own_off = off_ref[0].astype(F32)
    split_heads(k_ref, G, put_k)
    kbuf[me, pl.ds(R, 16), :] = jnp.full((16, D), own_off, F32).astype(BF16)
    split_heads(v_ref, G, put_v)
    pl.semaphore_wait(barrier, Z - 1 + (1 if Y == 2 else 0))

    def zcopy(buf, d, ss, rs, block):
        return pltpu.make_async_remote_copy(
            src_ref=buf.at[block], dst_ref=buf.at[block], send_sem=ss.at[d], recv_sem=rs.at[d],
            device_id=at(up(d), y), device_id_type=MESH)

    def ycopy(buf, d, ss, rs, block):
        return pltpu.make_async_remote_copy(
            src_ref=buf.at[block], dst_ref=buf.at[block], send_sem=ss.at[d], recv_sem=rs.at[d],
            device_id=at(z, other), device_id_type=MESH)

    def start_own(buf, zs, zr, ys, yr):
        if Y == 2:
            ycopy(buf, 0, ys, yr, me).start()
        for d in range(1, Z):
            zcopy(buf, d, zs, zr, me).start()

    def forward(buf, d, zs, zr, ys, yr):
        block = down(d) * Y + y
        zcopy(buf, d, zs, zr, block).wait_recv()
        if Y == 2:
            ycopy(buf, d, ys, yr, block).start()

    def arrive_y(buf, d, ys, yr):
        if Y == 2:
            ycopy(buf, d, ys, yr, down(d) * Y + other).wait_recv()

    start_own(kbuf, kz_s, kz_r, ky_s, ky_r)

    def put_q(h, x):
        qs[h // H, pl.ds((h % H) * T, T), :] = x.astype(BF16)

    split_heads(q_ref, G * H, put_q)

    def put_do(h, x):
        dos[h // H, pl.ds((h % H) * T, T), :] = x.astype(BF16)

    split_heads(do_ref, G * H, put_do)
    tmp[...] = do_ref[...].astype(F32) * fo_ref[...].astype(F32)
    for h in range(G * H):
        prod = tmp[pl.ds(h, T, stride=G * H), :]
        delta[h // H, :, pl.ds((h % H) * T, T)] = jnp.sum(prod.T, axis=0, keepdims=True)

    for d in range(1, Z):
        forward(kbuf, d, kz_s, kz_r, ky_s, ky_r)
    start_own(vbuf, vz_s, vz_r, vy_s, vy_r)
    for d in range(Z):
        arrive_y(kbuf, d, ky_s, ky_r)

    C = Y * T

    def key_rows(buf, c, g):
        return jnp.concatenate([buf[c * Y + i, pl.ds(g * T, T), :] for i in range(Y)], axis=0)

    lead = (lax.broadcasted_iota(jnp.int32, (T, Q), 0)
            - lax.broadcasted_iota(jnp.int32, (T, Q), 1) % T).astype(F32)

    def score_step(c, tops):
        new = []
        for g in range(G):
            s = dot_nt(key_rows(kbuf, c, g), qs[g]) * (scale * LOG2E)
            parts = []
            for i in range(Y):
                off = kbuf[c * Y + i, pl.ds(R, 16), :][0:1, :].astype(F32)
                gap = (own_off - off) * T
                gap = jnp.concatenate([gap] * (Q // D), axis=1)
                parts.append(jnp.where(lead <= gap, s[i * T:(i + 1) * T], -1e30))
            s = jnp.concatenate(parts, axis=0)
            s_scr[g, pl.ds(c * C, C), :] = s
            top = tops[g]
            top = jnp.maximum(top, jnp.max(s.reshape(C // 8, 8, Q), axis=0))
            new.append(top)
        return tuple(new)

    tops = lax.fori_loop(0, Z, score_step, tuple(jnp.full((8, Q), -1e30, F32) for _ in range(G)))
    tops = [jnp.max(t, axis=0, keepdims=True) for t in tops]
    if Z > 1:
        forward(vbuf, 1, vz_s, vz_r, vy_s, vy_r)

    def total_step(c, sums):
        new = []
        for g in range(G):
            e = jnp.exp2(s_scr[g, pl.ds(c * C, C), :] - tops[g])
            s_scr[g, pl.ds(c * C, C), :] = e
            new.append(sums[g] + jnp.sum(e.reshape(C // 8, 8, Q), axis=0))
        return tuple(new)

    sums = lax.fori_loop(0, Z, total_step, tuple(jnp.zeros((8, Q), F32) for _ in range(G)))
    inv = [1.0 / jnp.sum(t, axis=0, keepdims=True) for t in sums]
    for d in range(2, Z):
        forward(vbuf, d, vz_s, vz_r, vy_s, vy_r)

    def gycopy(ysend, yrecv, c, ss, rs):
        return pltpu.make_async_remote_copy(
            src_ref=ysend.at[c], dst_ref=yrecv.at[c], send_sem=ss.at[c], recv_sem=rs.at[c],
            device_id=at(z, other), device_id_type=MESH)

    def gzcopy(zsend, zrecv, d, ss, rs):
        return pltpu.make_async_remote_copy(
            src_ref=zsend.at[d], dst_ref=zrecv.at[d], send_sem=ss.at[d], recv_sem=rs.at[d],
            device_id=at(up(d), y), device_id_type=MESH)

    def keep_partial(x_buf, part, ysend, c, g):
        if Y == 2:
            part[c, pl.ds(g * T, T), :] = x_buf[pl.ds(y * T, T), :]
            ysend[c, pl.ds(g * T, T), :] = x_buf[pl.ds(other * T, T), :].astype(BF16)
        else:
            part[c, pl.ds(g * T, T), :] = x_buf[...]

    def value_step(i, carry):
        c = lax.rem(z + 1 + i, Z)
        for g in range(G):
            p = s_scr[g, pl.ds(c * C, C), :] * inv[g]
            s_scr[g, pl.ds(c * C, C), :] = p
            dqt[0:C, 0:D] = dot_nn(p.astype(BF16), dos[g])
            keep_partial(dqt.at[0:C, 0:D], partv, ysv, c, g)
        if Y == 2:
            gycopy(ysv, yrv, c, gvy_s, gvy_r).start()
        return carry

    lax.fori_loop(0, Z, value_step, 0)

    for d in range(Z):
        arrive_y(vbuf, d, vy_s, vy_r)

    def send_z(part, ysend, yrecv, zsend, zrecv, d, ys, yr, zs, zr):
        c = up(d)
        total = part[c]
        if Y == 2:
            gycopy(ysend, yrecv, c, ys, yr).wait_recv()
            total = total + yrecv[c].astype(F32)
        zsend[d] = total.astype(BF16)
        gzcopy(zsend, zrecv, d, zs, zr).start()

    for g in range(G):
        dqt[pl.ds(g * D, D), :] = jnp.zeros((D, Q), F32)
        kt[...] = jnp.zeros_like(kt)

    def key_chunk(c):
        for g in range(G):
            kc = key_rows(kbuf, c, g)
            dp = dot_nt(key_rows(vbuf, c, g), dos[g])
            ds = (s_scr[g, pl.ds(c * C, C), :] * (dp - delta[g])).astype(BF16)
            kt[...] = dot_nn(ds, qs[g]) * scale
            keep_partial(kt, partk, ysk, c, g)
            dqt[pl.ds(g * D, D), :] += dot_nn(kc.astype(F32).T.astype(BF16), ds)
        if Y == 2:
            gycopy(ysk, yrk, c, gky_s, gky_r).start()

    def key_step(i, carry):
        key_chunk(lax.rem(z + 1 + i, Z))
        send_z(partv, ysv, yrv, zsv, zrv, i + 1, gvy_s, gvy_r, gvz_s, gvz_r)
        return carry

    lax.fori_loop(0, Z - 1, key_step, 0)
    key_chunk(z)

    def send_k(i, carry):
        send_z(partk, ysk, yrk, zsk, zrk, i + 1, gky_s, gky_r, gkz_s, gkz_r)
        return carry

    lax.fori_loop(0, Z - 1, send_k, 0)

    for g in range(G):
        for h in range(H):
            dq_ref[pl.ds(g * H + h, T, stride=G * H), :] = (
                dqt[pl.ds(g * D, D), pl.ds(h * T, T)].T * scale)

    def finish(out, part, ysend, yrecv, zsend, zrecv, ys, yr, zs, zr):
        total = part[z]
        if Y == 2:
            gycopy(ysend, yrecv, z, ys, yr).wait_recv()
            total = total + yrecv[z].astype(F32)

        def add(d, acc):
            gzcopy(zsend, zrecv, d, zs, zr).wait_recv()
            return acc + zrecv[d].astype(F32)

        part[z] = lax.fori_loop(1, Z, add, total)
        for g in range(G):
            out[pl.ds(g, T, stride=G), :] = part[z, pl.ds(g * T, T), :]

    finish(dv_ref, partv, ysv, yrv, zsv, zrv, gvy_s, gvy_r, gvz_s, gvz_r)
    finish(dk_ref, partk, ysk, yrk, zsk, zrk, gky_s, gky_r, gkz_s, gkz_r)

    for d in range(Z):
        block = down(d) * Y + y
        if d > 0:
            zcopy(kbuf, d, kz_s, kz_r, me).wait_send()
            zcopy(vbuf, d, vz_s, vz_r, me).wait_send()
            gzcopy(zsv, zrv, d, gvz_s, gvz_r).wait_send()
            gzcopy(zsk, zrk, d, gkz_s, gkz_r).wait_send()
        if Y == 2:
            ycopy(kbuf, d, ky_s, ky_r, block).wait_send()
            ycopy(vbuf, d, vy_s, vy_r, block).wait_send()
            gycopy(ysv, yrv, d, gvy_s, gvy_r).wait_send()
            gycopy(ysk, yrk, d, gky_s, gky_r).wait_send()


def on_device(Y, query_vectors, key_vectors, value_rows, forward_out, out_grad, block_offsets):
    T, QH, D = query_vectors.shape
    G = key_vectors.shape[1]
    H = QH // G
    N = lax.axis_size("ctx")
    Z = N // Y
    R, Q, C = G * T, H * T, Y * T
    vmem = pl.BlockSpec(memory_space=pltpu.VMEM)
    smem = pl.BlockSpec(memory_space=pltpu.SMEM)
    blocks = lambda dt: pltpu.VMEM((Z, R, D), dt)
    dq, dk, dv = pl.pallas_call(
        functools.partial(kernel, Z, Y, G, H, T, D),
        out_shape=(
            jax.ShapeDtypeStruct((T * QH, D), F32),
            jax.ShapeDtypeStruct((R, D), F32),
            jax.ShapeDtypeStruct((R, D), F32),
        ),
        in_specs=[vmem] * 5 + [smem],
        out_specs=[vmem] * 3,
        scratch_shapes=[
            pltpu.VMEM((T * QH, D), F32),
            pltpu.VMEM((G, Q, D), BF16),
            pltpu.VMEM((G, Q, D), BF16),
            pltpu.VMEM((N, R + 16, D), BF16),
            pltpu.VMEM((N, R, D), BF16),
            pltpu.VMEM((C, D), F32),
            pltpu.VMEM((G, N * T, Q), F32),
            pltpu.VMEM((G, 1, Q), F32),
            pltpu.VMEM((G * D, Q), F32),
            blocks(F32), blocks(F32),
            blocks(BF16), blocks(BF16), blocks(BF16), blocks(BF16),
            blocks(BF16), blocks(BF16), blocks(BF16), blocks(BF16),
        ] + [pltpu.SemaphoreType.DMA((Z,))] * 16,
        compiler_params=pltpu.CompilerParams(
            collective_id=0, has_side_effects=True, vmem_limit_bytes=48 * 1024 * 1024
        ),
        cost_estimate=pl.CostEstimate(
            flops=10 * G * Q * N * T * D, bytes_accessed=4 * T * QH * D * 4,
            transcendentals=G * Q * N * T,
        ),
    )(
        query_vectors.reshape(T * QH, D), key_vectors.reshape(R, D), value_rows.reshape(R, D),
        forward_out.reshape(T * QH, D), out_grad.reshape(T * QH, D), block_offsets,
    )
    return dq.reshape(T, QH, D), dk.reshape(T, G, D), dv.reshape(T, G, D)


def solution(mesh):
    pair = 2 if mesh.shape["groups"] == 2 and mesh.shape["ctx"] % 2 == 0 else 1
    tokens = P(("groups", "ctx"), "heads", None)
    return jax.shard_map(
        functools.partial(on_device, pair), mesh=mesh,
        in_specs=(tokens,) * 5 + (P(("groups", "ctx")),),
        out_specs=(tokens,) * 3, check_vma=False,
    )
```

```python
import functools

import jax
import jax.numpy as jnp
from jax import lax
from jax.experimental import pallas as pl
from jax.experimental.pallas import tpu as pltpu
from jax.sharding import PartitionSpec as P

MESH = pl.DeviceIdType.MESH
LOG2E = 1.4426950408889634
F32 = jnp.float32
BF16 = jnp.bfloat16
PAD = 16


def dot_nt(a, b):
    return lax.dot_general(a, b, (((1,), (1,)), ((), ())), preferred_element_type=F32)


def dot_nn(a, b):
    return lax.dot_general(a, b, (((1,), (0,)), ((), ())), preferred_element_type=F32)


def loop(n, body):
    if n <= 4:
        for i in range(n):
            body(i)
    else:
        def step(i, carry):
            body(i)
            return carry
        lax.fori_loop(0, n, step, 0)


def kernel(Z, Y, G, H, T, D, *refs):
    (q_hbm, k_hbm, v_hbm, fo_hbm, do_hbm, off_ref, dq_ref, dk_ref, dv_ref,
     q_ref, k_ref, v_ref, fo_ref, do_ref, in_sem,
     tmp, qs, dos, qst, dost, kst, vst, delta, delst, kbuf, vbuf,
     s_scr, ds_scr, top_scr, partv, partk,
     rsv, lsv, rrv, lrv, rsk, lsk, rrk, lrk,
     dqst, dqr, gst, gr, ys, yr,
     kr_s, kr_r, kl_s, kl_r, vr_s, vr_r, vl_s, vl_r,
     grv_s, grv_r, glv_s, glv_r, grk_s, grk_r, glk_s, glk_r) = refs
    me = lax.axis_index("ctx")
    z, y = me // Y, me % Y
    other = 1 - y if Y == 2 else 0
    scale = D ** (-0.5)
    GL = G // Y
    C = Y * T
    CP = Y * (T + PAD)
    HT = H * T
    Q = Y * HT
    first = y * GL
    theirs = other * GL

    def at(zz, yy):
        return {"ctx": zz * Y + yy}

    inputs = [(k_hbm, k_ref), (q_hbm, q_ref), (v_hbm, v_ref), (do_hbm, do_ref), (fo_hbm, fo_ref)]
    loads = [pltpu.make_async_copy(a, b, in_sem.at[i]) for i, (a, b) in enumerate(inputs)]
    for cp in loads:
        cp.start()

    barrier = pltpu.get_barrier_semaphore()

    @pl.when(z > 0)
    def _():
        pl.semaphore_signal(barrier, inc=1, device_id=at(z - 1, y), device_id_type=MESH)

    @pl.when(z < Z - 1)
    def _():
        pl.semaphore_signal(barrier, inc=1, device_id=at(z + 1, y), device_id_type=MESH)

    if Y == 2:
        pl.semaphore_signal(barrier, inc=1, device_id=at(z, other), device_id_type=MESH)

    def head(src, heads, h):
        return tmp[pl.ds(h, T, stride=heads), :]

    def aligned(x):
        return pl.multiple_of(x, 16)

    def ycopy(i, src, dst):
        return pltpu.make_async_remote_copy(
            src_ref=src, dst_ref=dst, send_sem=ys.at[i], recv_sem=yr.at[i],
            device_id=at(z, other), device_id_type=MESH)

    own_rows = pl.ds(aligned(y * HT), HT)
    own_keys = pl.ds(aligned(y * (T + PAD)), T + PAD)
    own_vals = pl.ds(aligned(y * T), T)
    own_lanes = pl.ds(pl.multiple_of(y * HT, 128), HT)
    y_copies = []
    if Y == 2:
        y_copies = [
            ycopy(0, kst, kbuf.at[z, :, own_keys]),
            ycopy(1, qst, qs.at[:, own_rows]),
            ycopy(2, vst, vbuf.at[z, :, own_vals]),
            ycopy(3, dost, dos.at[:, own_rows]),
            ycopy(4, delst, delta.at[:, :, own_lanes]),
            ycopy(5, dqst, dqr),
            ycopy(6, gst.at[0], gr.at[0]),
            ycopy(7, gst.at[1], gr.at[1]),
        ]

    def y_start(i):
        if Y == 2:
            y_copies[i].start()

    def y_wait(i):
        if Y == 2:
            y_copies[i].wait_recv()

    def ag_copies(buf, s, sems):
        rs, rr, ls, lr = sems
        right = pltpu.make_async_remote_copy(
            src_ref=buf.at[jnp.maximum(z - s, 0)], dst_ref=buf.at[jnp.maximum(z - s, 0)],
            send_sem=rs.at[s], recv_sem=rr.at[s],
            device_id=at(jnp.minimum(z + 1, Z - 1), y), device_id_type=MESH)
        left = pltpu.make_async_remote_copy(
            src_ref=buf.at[jnp.minimum(z + s, Z - 1)], dst_ref=buf.at[jnp.minimum(z + s, Z - 1)],
            send_sem=ls.at[s], recv_sem=lr.at[s],
            device_id=at(jnp.maximum(z - 1, 0), y), device_id_type=MESH)
        return right, left

    def ag_has(s):
        return (z - s >= 0) & (z < Z - 1), (z + s < Z) & (z > 0)

    def ag_send(buf, s, sems):
        right, left = ag_copies(buf, s, sems)
        has_right, has_left = ag_has(s)
        pl.when(has_right)(right.start)
        pl.when(has_left)(left.start)

    def ag_wait_send(buf, s, sems):
        right, left = ag_copies(buf, s, sems)
        has_right, has_left = ag_has(s)
        pl.when(has_right)(right.wait_send)
        pl.when(has_left)(left.wait_send)

    def ag_recv(buf, s, sems):
        right, left = ag_copies(buf, s, sems)
        pl.when(z - 1 - s >= 0)(right.wait_recv)
        pl.when(z + 1 + s < Z)(left.wait_recv)

    k_sems = (kr_s, kr_r, kl_s, kl_r)
    v_sems = (vr_s, vr_r, vl_s, vl_r)

    own_off = off_ref[0].astype(F32)
    off_rows = jnp.full((PAD, D), own_off, F32).astype(BF16)
    loads[0].wait()
    tmp[0:T * G, :] = k_ref[...].astype(F32)
    for i in range(GL):
        kbuf[z, i, pl.ds(aligned(y * (T + PAD)), T), :] = head(tmp, G, first + i).astype(BF16)
        kbuf[z, i, pl.ds(aligned(y * (T + PAD) + T), PAD), :] = off_rows
        if Y == 2:
            kst[i, 0:T, :] = head(tmp, G, theirs + i).astype(BF16)
            kst[i, T:T + PAD, :] = off_rows
    pl.semaphore_wait(barrier, (z > 0).astype(jnp.int32) + (z < Z - 1).astype(jnp.int32) + (Y - 1))
    y_start(0)

    def split_queries(dst, stage):
        for i in range(GL):
            for h in range(H):
                if Y == 2:
                    stage[i, pl.ds(h * T, T), :] = head(tmp, G * H, (theirs + i) * H + h).astype(BF16)
                dst[i, pl.ds(aligned(y * HT + h * T), T), :] = (
                    head(tmp, G * H, (first + i) * H + h).astype(BF16))

    loads[1].wait()
    tmp[...] = q_ref[...].astype(F32)
    split_queries(qs, qst)
    y_start(1)
    y_wait(0)
    ag_send(kbuf, 0, k_sems)

    loads[2].wait()
    tmp[0:T * G, :] = v_ref[...].astype(F32)
    for i in range(GL):
        vbuf[z, i, own_vals, :] = head(tmp, G, first + i).astype(BF16)
        if Y == 2:
            vst[i] = head(tmp, G, theirs + i).astype(BF16)
    y_start(2)
    loads[3].wait()
    tmp[...] = do_ref[...].astype(F32)
    split_queries(dos, dost)
    y_start(3)

    ag_recv(kbuf, 0, k_sems)
    if Z > 2:
        ag_send(kbuf, 1, k_sems)

    loads[4].wait()
    tmp[...] = do_ref[...].astype(F32) * fo_ref[...].astype(F32)
    for i in range(GL):
        for h in range(H):
            def lanes(g):
                return jnp.sum(head(tmp, G * H, g * H + h).T, axis=0, keepdims=True)
            delta[i, :, pl.ds(pl.multiple_of(y * HT + h * T, 128), T)] = lanes(first + i)
            if Y == 2:
                delst[i, :, pl.ds(h * T, T)] = lanes(theirs + i)
    y_start(4)

    def key_rows(c, g):
        return jnp.concatenate([kbuf[c, g, pl.ds(i * (T + PAD), T), :] for i in range(Y)], axis=0)

    def block_off(c, i):
        return kbuf[c, 0, pl.ds(i * (T + PAD) + T, PAD), :][0:1, :].astype(F32)

    lead = (lax.broadcasted_iota(jnp.int32, (T, Q), 0)
            - lax.broadcasted_iota(jnp.int32, (T, Q), 1) % T).astype(F32)
    top_scr[...] = jnp.full(top_scr.shape, -1e30, F32)
    y_wait(1)
    q_off = jnp.concatenate([block_off(z, i) for i in range(Y) for h in range(H)], axis=1)

    def scores(c):
        for g in range(GL):
            s = dot_nt(key_rows(c, g), qs[g]) * (scale * LOG2E)
            parts = []
            for i in range(Y):
                off = jnp.concatenate([block_off(c, i)] * (Q // D), axis=1)
                parts.append(jnp.where(lead <= (q_off - off) * T, s[i * T:(i + 1) * T], -1e30))
            s = jnp.concatenate(parts, axis=0)
            s_scr[g, pl.ds(pl.multiple_of(c * C, 128), C), :] = s
            top_scr[g] = jnp.maximum(top_scr[g], jnp.max(s.reshape(C // 8, 8, Q), axis=0))

    def scores_at(s):
        pl.when(z - 1 - s >= 0)(lambda: scores(z - 1 - s))
        pl.when(z + 1 + s < Z)(lambda: scores(z + 1 + s))

    scores(z)

    def key_arrival(s):
        ag_recv(kbuf, s, k_sems)
        if not isinstance(s, int):
            pl.when(s < Z - 2)(lambda: ag_send(kbuf, s + 1, k_sems))
        elif s < Z - 2:
            ag_send(kbuf, s + 1, k_sems)
        scores_at(s)

    scores_at(0)
    loop(Z - 3, lambda i: key_arrival(i + 1))
    ag_recv(kbuf, Z - 2, k_sems)
    y_wait(2)
    ag_send(vbuf, 0, v_sems)
    scores_at(Z - 2)

    tops = [jnp.max(top_scr[g], axis=0, keepdims=True) for g in range(GL)]
    ag_recv(vbuf, 0, v_sems)
    ag_send(vbuf, 1, v_sems)

    def total_step(c, sums):
        new = []
        for g in range(GL):
            rows = pl.ds(pl.multiple_of(c * C, 128), C)
            e = jnp.exp2(s_scr[g, rows, :] - tops[g])
            s_scr[g, rows, :] = e
            new.append(sums[g] + jnp.sum(e.reshape(C // 8, 8, Q), axis=0))
        return tuple(new)

    sums = lax.fori_loop(0, Z, total_step, tuple(jnp.zeros((8, Q), F32) for _ in range(GL)))
    inv = [1.0 / jnp.sum(t, axis=0, keepdims=True) for t in sums]

    def value_arrival(s):
        ag_recv(vbuf, s, v_sems)
        if not isinstance(s, int):
            pl.when(s < Z - 2)(lambda: ag_send(vbuf, s + 1, v_sems))
        elif s < Z - 2:
            ag_send(vbuf, s + 1, v_sems)

    loop(Z - 3, lambda i: value_arrival(i + 1))
    y_wait(3)

    def rs_copies(j, bufs, sems):
        rsend, lsend, rrecv, lrecv = bufs
        rs, rr, ls, lr = sems
        right = pltpu.make_async_remote_copy(
            src_ref=rsend.at[j], dst_ref=rrecv.at[j], send_sem=rs.at[j], recv_sem=rr.at[j],
            device_id=at(jnp.minimum(z + 1, Z - 1), y), device_id_type=MESH)
        left = pltpu.make_async_remote_copy(
            src_ref=lsend.at[j], dst_ref=lrecv.at[j], send_sem=ls.at[j], recv_sem=lr.at[j],
            device_id=at(jnp.maximum(z - 1, 0), y), device_id_type=MESH)
        return right, left

    def rs_first(j, part, bufs, sems):
        right, left = rs_copies(j, bufs, sems)

        @pl.when(z == 0)
        def _():
            bufs[0][j] = part[Z - 1 - j].astype(BF16)
            right.start()

        @pl.when(z == Z - 1)
        def _():
            bufs[1][j] = part[j].astype(BF16)
            left.start()

    def rs_relay(j, part, bufs, sems):
        right, left = rs_copies(j, bufs, sems)

        @pl.when((z > 0) & (z < Z - 1 - j))
        def _():
            right.wait_recv()
            bufs[0][j] = (part[Z - 1 - j] + bufs[2][j].astype(F32)).astype(BF16)
            right.start()

        @pl.when((z < Z - 1) & (z > j))
        def _():
            left.wait_recv()
            bufs[1][j] = (part[j] + bufs[3][j].astype(F32)).astype(BF16)
            left.start()

    def rs_wait_send(j, bufs, sems):
        right, left = rs_copies(j, bufs, sems)
        pl.when(z < Z - 1 - j)(right.wait_send)
        pl.when(z > j)(left.wait_send)

    bufs_v, sems_v = (rsv, lsv, rrv, lrv), (grv_s, grv_r, glv_s, glv_r)
    bufs_k, sems_k = (rsk, lsk, rrk, lrk), (grk_s, grk_r, glk_s, glk_r)
    half = Z // 2

    def value_chunk(c):
        rows = pl.ds(pl.multiple_of(c * C, 128), C)
        for g in range(GL):
            p = s_scr[g, rows, :] * inv[g]
            s_scr[g, rows, :] = p
            partv[c, pl.ds(g * C, C), :] = dot_nn(p.astype(BF16), dos[g])

    def value_pair(j):
        value_chunk(Z - 1 - j)
        value_chunk(j)
        rs_first(j, partv, bufs_v, sems_v)

    loop(half, value_pair)
    loop(Z - 1 - half, lambda i: rs_first(half + i, partv, bufs_v, sems_v))

    ag_recv(vbuf, Z - 2, v_sems)
    y_wait(4)

    def key_chunk(c):
        rows = pl.ds(pl.multiple_of(c * C, 128), C)
        for g in range(GL):
            dp = dot_nt(vbuf[c, g], dos[g])
            ds = (s_scr[g, rows, :] * (dp - delta[g])).astype(BF16)
            ds_scr[g, rows, :] = ds
            partk[c, pl.ds(g * C, C), :] = dot_nn(ds, qs[g]) * scale

    def key_pair(j):
        key_chunk(Z - 1 - j)
        key_chunk(j)
        rs_first(j, partk, bufs_k, sems_k)
        rs_relay(j, partv, bufs_v, sems_v)

    loop(half, key_pair)
    loop(Z - 1 - half, lambda i: rs_first(half + i, partk, bufs_k, sems_k))
    loop(Z - 1 - half, lambda i: rs_relay(half + i, partv, bufs_v, sems_v))

    rs_relay(0, partk, bufs_k, sems_k)
    own_dq = []
    for g in range(GL):
        kt = jnp.concatenate(
            [key_rows(c, g).astype(F32).T.astype(BF16) for c in range(Z)], axis=1)
        tmp_rows = pl.ds(0, D)
        dqt = dot_nn(kt, ds_scr[g]) * scale
        for i in range(Y):
            for h in range(H):
                block = dqt[:, (i * H + h) * T:(i * H + h + 1) * T].T

                def keep(block=block, h=h):
                    dq_ref[pl.ds((first + g) * H + h, T, stride=G * H), :] = block

                def stage(block=block, h=h):
                    dqst[g, pl.ds(h * T, T), :] = block.astype(BF16)

                if Y == 2:
                    pl.when(y == i)(keep)
                    pl.when(y != i)(stage)
                else:
                    keep()
    y_start(5)

    def finish(part, bufs, sems, slot):
        for s in range(2):
            @pl.when(z > 0 if s == 0 else z < Z - 1)
            def _():
                j = jnp.clip(Z - 1 - z if s == 0 else z, 0, Z - 2)
                rs_copies(j, bufs, sems)[s].wait_recv()
                part[z] = part[z] + bufs[2 + s][j].astype(F32)
        if Y == 2:
            for g in range(GL):
                gst[slot, g] = part[z, pl.ds(aligned(g * C + other * T), T), :].astype(BF16)
        y_start(6 + slot)

    def put(out, part, slot):
        for g in range(GL):
            out[pl.ds(first + g, T, stride=G), :] = part[z, pl.ds(aligned(g * C + y * T), T), :]
        y_wait(6 + slot)
        if Y == 2:
            for g in range(GL):
                out[pl.ds(theirs + g, T, stride=G), :] = gr[slot, g].astype(F32)

    if Z > 2:
        rs_relay(1, partk, bufs_k, sems_k)
    finish(partv, bufs_v, sems_v, 0)
    loop(Z - 3, lambda i: rs_relay(2 + i, partk, bufs_k, sems_k))
    put(dv_ref, partv, 0)
    y_wait(5)
    if Y == 2:
        for g in range(GL):
            for h in range(H):
                dq_ref[pl.ds((theirs + g) * H + h, T, stride=G * H), :] = (
                    dqr[g, pl.ds(h * T, T), :].astype(F32))
    finish(partk, bufs_k, sems_k, 1)
    put(dk_ref, partk, 1)

    def drain(s):
        ag_wait_send(kbuf, s, k_sems)
        ag_wait_send(vbuf, s, v_sems)
        rs_wait_send(s, bufs_v, sems_v)
        rs_wait_send(s, bufs_k, sems_k)

    loop(Z - 1, drain)
    for cp in y_copies:
        cp.wait_send()


def on_device(Y, query_vectors, key_vectors, value_rows, forward_out, out_grad, block_offsets):
    T, QH, D = query_vectors.shape
    G = key_vectors.shape[1]
    H = QH // G
    N = lax.axis_size("ctx")
    Z = N // Y
    GL, C, HT, R = G // Y, Y * T, H * T, T * G
    Q = Y * HT
    vmem = pl.BlockSpec(memory_space=pltpu.VMEM)
    smem = pl.BlockSpec(memory_space=pltpu.SMEM)
    hbm = pl.BlockSpec(memory_space=pltpu.HBM)
    V = pltpu.VMEM
    part = V((Z, GL * C, D), F32)
    wire = V((Z - 1, GL * C, D), BF16)
    dq, dk, dv = pl.pallas_call(
        functools.partial(kernel, Z, Y, G, H, T, D),
        out_shape=(
            jax.ShapeDtypeStruct((T * QH, D), F32),
            jax.ShapeDtypeStruct((R, D), F32),
            jax.ShapeDtypeStruct((R, D), F32),
        ),
        in_specs=[hbm] * 5 + [smem],
        out_specs=[vmem] * 3,
        scratch_shapes=[
            V((T * QH, D), BF16), V((R, D), BF16), V((R, D), BF16),
            V((T * QH, D), BF16), V((T * QH, D), BF16), pltpu.SemaphoreType.DMA((5,)),
            V((T * QH, D), F32),
            V((GL, Q, D), BF16), V((GL, Q, D), BF16),
            V((GL, HT, D), BF16), V((GL, HT, D), BF16),
            V((GL, T + PAD, D), BF16), V((GL, T, D), BF16),
            V((GL, 1, Q), F32), V((GL, 1, HT), F32),
            V((Z, GL, Y * (T + PAD), D), BF16), V((Z, GL, C, D), BF16),
            V((GL, N * T, Q), F32), V((GL, N * T, Q), BF16), V((GL, 8, Q), F32),
            part, part, wire, wire, wire, wire, wire, wire, wire, wire,
            V((GL, HT, D), BF16), V((GL, HT, D), BF16),
            V((2, GL, T, D), BF16), V((2, GL, T, D), BF16),
            pltpu.SemaphoreType.DMA((8,)), pltpu.SemaphoreType.DMA((8,)),
        ] + [pltpu.SemaphoreType.DMA((Z - 1,))] * 16,
        compiler_params=pltpu.CompilerParams(
            collective_id=0, has_side_effects=True, vmem_limit_bytes=56 * 1024 * 1024
        ),
        cost_estimate=pl.CostEstimate(
            flops=10 * GL * Q * N * T * D, bytes_accessed=4 * T * QH * D * 4,
            transcendentals=GL * Q * N * T,
        ),
    )(
        query_vectors.reshape(T * QH, D), key_vectors.reshape(R, D), value_rows.reshape(R, D),
        forward_out.reshape(T * QH, D), out_grad.reshape(T * QH, D), block_offsets,
    )
    return dq.reshape(T, QH, D), dk.reshape(T, G, D), dv.reshape(T, G, D)


def solution(mesh):
    pair = 2 if mesh.shape["groups"] == 2 and mesh.shape["ctx"] % 2 == 0 else 1
    tokens = P(("groups", "ctx"), "heads", None)
    return jax.shard_map(
        functools.partial(on_device, pair), mesh=mesh,
        in_specs=(tokens,) * 5 + (P(("groups", "ctx")),),
        out_specs=(tokens,) * 3, check_vma=False,
    )
```

```python
import functools

import jax
import jax.numpy as jnp
from jax import lax
from jax.experimental import pallas as pl
from jax.experimental.pallas import tpu as pltpu
from jax.sharding import PartitionSpec as P

MESH = pl.DeviceIdType.MESH
LOG2E = 1.4426950408889634
F32 = jnp.float32
BF16 = jnp.bfloat16
PAD = 16


def dot_nt(a, b):
    return lax.dot_general(a, b, (((1,), (1,)), ((), ())), preferred_element_type=F32)


def dot_nn(a, b):
    return lax.dot_general(a, b, (((1,), (0,)), ((), ())), preferred_element_type=F32)


def loop(n, body):
    if n <= 4:
        for i in range(n):
            body(i)
    else:
        def step(i, carry):
            body(i)
            return carry
        lax.fori_loop(0, n, step, 0)


def kernel(Z, Y, G, H, T, D, *refs):
    (q_hbm, k_hbm, v_hbm, fo_hbm, do_hbm, off_ref, dq_ref, dk_ref, dv_ref,
     q_ref, k_ref, v_ref, fo_ref, do_ref, in_sem,
     tmp, qs, dos, qst, dost, kst, vst, delta, delst, kbuf, vbuf,
     s_scr, ds_scr, top_scr, partv, partk,
     gsv, grv, gsk, grk,
     dqst, dqr, gst, gr, ys, yr,
     ks_s, ks_r, vs_s, vs_r, gv_s, gv_r, gk_s, gk_r) = refs
    me = lax.axis_index("ctx")
    z, y = me // Y, me % Y
    other = 1 - y if Y == 2 else 0
    scale = D ** (-0.5)
    GL = G // Y
    C = Y * T
    CP = Y * (T + PAD)
    HT = H * T
    Q = Y * HT
    first = y * GL
    theirs = other * GL

    def at(zz, yy):
        return {"ctx": zz * Y + yy}

    inputs = [(k_hbm, k_ref), (q_hbm, q_ref), (v_hbm, v_ref), (do_hbm, do_ref), (fo_hbm, fo_ref)]
    loads = [pltpu.make_async_copy(a, b, in_sem.at[i]) for i, (a, b) in enumerate(inputs)]
    for cp in loads:
        cp.start()

    barrier = pltpu.get_barrier_semaphore()

    for d in range(1, Z):
        pl.semaphore_signal(
            barrier, inc=1, device_id=at(lax.rem(z + d, Z), y), device_id_type=MESH)
    if Y == 2:
        pl.semaphore_signal(barrier, inc=1, device_id=at(z, other), device_id_type=MESH)

    def head(src, heads, h):
        return tmp[pl.ds(h, T, stride=heads), :]

    def aligned(x):
        return pl.multiple_of(x, 16)

    def ycopy(i, src, dst):
        return pltpu.make_async_remote_copy(
            src_ref=src, dst_ref=dst, send_sem=ys.at[i], recv_sem=yr.at[i],
            device_id=at(z, other), device_id_type=MESH)

    own_rows = pl.ds(aligned(y * HT), HT)
    own_keys = pl.ds(aligned(y * (T + PAD)), T + PAD)
    own_vals = pl.ds(aligned(y * T), T)
    own_lanes = pl.ds(pl.multiple_of(y * HT, 128), HT)
    y_copies = []
    if Y == 2:
        y_copies = [
            ycopy(0, kst, kbuf.at[z, :, own_keys]),
            ycopy(1, qst, qs.at[:, own_rows]),
            ycopy(2, vst, vbuf.at[z, :, own_vals]),
            ycopy(3, dost, dos.at[:, own_rows]),
            ycopy(4, delst, delta.at[:, :, own_lanes]),
            ycopy(5, dqst, dqr),
            ycopy(6, gst.at[0], gr.at[0]),
            ycopy(7, gst.at[1], gr.at[1]),
        ]

    def y_start(i):
        if Y == 2:
            y_copies[i].start()

    def y_wait(i):
        if Y == 2:
            y_copies[i].wait_recv()

    def mate(i, near=True):
        if not near:
            i = Z - 2 - i
        up = i + jnp.where(i >= z, 1, 0)
        v = Z - 1 - i
        return jnp.where(z < Z // 2, up, v - jnp.where(v <= z, 1, 0))

    def ag_copy(buf, t, block, sems):
        return pltpu.make_async_remote_copy(
            src_ref=buf.at[block], dst_ref=buf.at[block],
            send_sem=sems[0].at[t], recv_sem=sems[1].at[block],
            device_id=at(t, y), device_id_type=MESH)

    def ag_send(buf, sems):
        loop(Z - 1, lambda i: ag_copy(buf, mate(i), z, sems).start())

    def ag_recv(buf, i, sems):
        ag_copy(buf, mate(i), mate(i), sems).wait_recv()

    k_sems = (ks_s, ks_r)
    v_sems = (vs_s, vs_r)

    own_off = off_ref[0].astype(F32)
    off_rows = jnp.full((PAD, D), own_off, F32).astype(BF16)
    loads[0].wait()
    tmp[0:T * G, :] = k_ref[...].astype(F32)
    for i in range(GL):
        kbuf[z, i, pl.ds(aligned(y * (T + PAD)), T), :] = head(tmp, G, first + i).astype(BF16)
        kbuf[z, i, pl.ds(aligned(y * (T + PAD) + T), PAD), :] = off_rows
        if Y == 2:
            kst[i, 0:T, :] = head(tmp, G, theirs + i).astype(BF16)
            kst[i, T:T + PAD, :] = off_rows
    pl.semaphore_wait(barrier, Z - 1 + Y - 1)
    y_start(0)

    def split_queries(dst, stage):
        for i in range(GL):
            for h in range(H):
                if Y == 2:
                    stage[i, pl.ds(h * T, T), :] = head(tmp, G * H, (theirs + i) * H + h).astype(BF16)
                dst[i, pl.ds(aligned(y * HT + h * T), T), :] = (
                    head(tmp, G * H, (first + i) * H + h).astype(BF16))

    loads[1].wait()
    tmp[...] = q_ref[...].astype(F32)
    split_queries(qs, qst)
    y_start(1)
    y_wait(0)
    ag_send(kbuf, k_sems)

    loads[2].wait()
    tmp[0:T * G, :] = v_ref[...].astype(F32)
    for i in range(GL):
        vbuf[z, i, own_vals, :] = head(tmp, G, first + i).astype(BF16)
        if Y == 2:
            vst[i] = head(tmp, G, theirs + i).astype(BF16)
    y_start(2)
    loads[3].wait()
    tmp[...] = do_ref[...].astype(F32)
    split_queries(dos, dost)
    y_start(3)

    loads[4].wait()
    tmp[...] = do_ref[...].astype(F32) * fo_ref[...].astype(F32)
    for i in range(GL):
        for h in range(H):
            def lanes(g):
                return jnp.sum(head(tmp, G * H, g * H + h).T, axis=0, keepdims=True)
            delta[i, :, pl.ds(pl.multiple_of(y * HT + h * T, 128), T)] = lanes(first + i)
            if Y == 2:
                delst[i, :, pl.ds(h * T, T)] = lanes(theirs + i)
    y_start(4)

    def key_rows(c, g):
        return jnp.concatenate([kbuf[c, g, pl.ds(i * (T + PAD), T), :] for i in range(Y)], axis=0)

    def block_off(c, i):
        return kbuf[c, 0, pl.ds(i * (T + PAD) + T, PAD), :][0:1, :].astype(F32)

    lead = (lax.broadcasted_iota(jnp.int32, (T, Q), 0)
            - lax.broadcasted_iota(jnp.int32, (T, Q), 1) % T).astype(F32)
    top_scr[...] = jnp.full(top_scr.shape, -1e30, F32)
    y_wait(1)
    q_off = jnp.concatenate([block_off(z, i) for i in range(Y) for h in range(H)], axis=1)

    def scores(c):
        for g in range(GL):
            s = dot_nt(key_rows(c, g), qs[g]) * (scale * LOG2E)
            parts = []
            for i in range(Y):
                off = jnp.concatenate([block_off(c, i)] * (Q // D), axis=1)
                parts.append(jnp.where(lead <= (q_off - off) * T, s[i * T:(i + 1) * T], -1e30))
            s = jnp.concatenate(parts, axis=0)
            s_scr[g, pl.ds(pl.multiple_of(c * C, 128), C), :] = s
            top_scr[g] = jnp.maximum(top_scr[g], jnp.max(s.reshape(C // 8, 8, Q), axis=0))

    scores(z)
    y_wait(2)
    ag_send(vbuf, v_sems)

    def key_arrival(i):
        ag_recv(kbuf, i, k_sems)
        scores(mate(i))

    loop(Z - 1, key_arrival)

    tops = [jnp.max(top_scr[g], axis=0, keepdims=True) for g in range(GL)]

    def total_step(c, sums):
        new = []
        for g in range(GL):
            rows = pl.ds(pl.multiple_of(c * C, 128), C)
            e = jnp.exp2(s_scr[g, rows, :] - tops[g])
            s_scr[g, rows, :] = e
            new.append(sums[g] + jnp.sum(e.reshape(C // 8, 8, Q), axis=0))
        return tuple(new)

    sums = lax.fori_loop(0, Z, total_step, tuple(jnp.zeros((8, Q), F32) for _ in range(GL)))
    inv = [1.0 / jnp.sum(t, axis=0, keepdims=True) for t in sums]

    y_wait(3)

    def rs_copy(c, src, bufs, sems):
        return pltpu.make_async_remote_copy(
            src_ref=bufs[0].at[c], dst_ref=bufs[1].at[src],
            send_sem=sems[0].at[c], recv_sem=sems[1].at[src],
            device_id=at(c, y), device_id_type=MESH)

    bufs_v, sems_v = (gsv, grv), (gv_s, gv_r)
    bufs_k, sems_k = (gsk, grk), (gk_s, gk_r)

    def value_chunk(c, put):
        rows = pl.ds(pl.multiple_of(c * C, 128), C)
        for g in range(GL):
            p = s_scr[g, rows, :] * inv[g]
            s_scr[g, rows, :] = p
            put(g, dot_nn(p.astype(BF16), dos[g]))

    def key_chunk(c, put):
        rows = pl.ds(pl.multiple_of(c * C, 128), C)
        for g in range(GL):
            dp = dot_nt(vbuf[c, g], dos[g])
            ds = (s_scr[g, rows, :] * (dp - delta[g])).astype(BF16)
            ds_scr[g, rows, :] = ds
            put(g, dot_nn(ds, qs[g]) * scale)

    def send_chunk(i, chunk, bufs, sems):
        c = mate(i, False)

        def put(g, x):
            bufs[0][c, pl.ds(g * C, C), :] = x.astype(BF16)

        chunk(c, put)
        rs_copy(c, z, bufs, sems).start()

    def own_chunk(chunk, part):
        def put(g, x):
            part[pl.ds(g * C, C), :] = x

        chunk(z, put)

    loop(Z - 1, lambda i: send_chunk(i, value_chunk, bufs_v, sems_v))
    own_chunk(value_chunk, partv)
    y_wait(4)
    loop(Z - 1, lambda i: ag_recv(vbuf, i, v_sems))
    loop(Z - 1, lambda i: send_chunk(i, key_chunk, bufs_k, sems_k))
    own_chunk(key_chunk, partk)

    for g in range(GL):
        kt = jnp.concatenate(
            [key_rows(c, g).astype(F32).T.astype(BF16) for c in range(Z)], axis=1)
        dqt = dot_nn(kt, ds_scr[g]) * scale
        for i in range(Y):
            for h in range(H):
                block = dqt[:, (i * H + h) * T:(i * H + h + 1) * T].T

                def keep(block=block, h=h):
                    dq_ref[pl.ds((first + g) * H + h, T, stride=G * H), :] = block

                def stage(block=block, h=h):
                    dqst[g, pl.ds(h * T, T), :] = block.astype(BF16)

                if Y == 2:
                    pl.when(y == i)(keep)
                    pl.when(y != i)(stage)
                else:
                    keep()
    y_start(5)

    def finish(part, bufs, sems, slot):
        def add(i):
            rs_copy(z, mate(i), bufs, sems).wait_recv()
            part[...] += bufs[1][mate(i)].astype(F32)

        loop(Z - 1, add)
        if Y == 2:
            for g in range(GL):
                gst[slot, g] = part[pl.ds(aligned(g * C + other * T), T), :].astype(BF16)
        y_start(6 + slot)

    def put(out, part, slot):
        for g in range(GL):
            out[pl.ds(first + g, T, stride=G), :] = part[pl.ds(aligned(g * C + y * T), T), :]
        y_wait(6 + slot)
        if Y == 2:
            for g in range(GL):
                out[pl.ds(theirs + g, T, stride=G), :] = gr[slot, g].astype(F32)

    finish(partv, bufs_v, sems_v, 0)
    put(dv_ref, partv, 0)
    y_wait(5)
    if Y == 2:
        for g in range(GL):
            for h in range(H):
                dq_ref[pl.ds((theirs + g) * H + h, T, stride=G * H), :] = (
                    dqr[g, pl.ds(h * T, T), :].astype(F32))
    finish(partk, bufs_k, sems_k, 1)
    put(dk_ref, partk, 1)

    def drain(i):
        t = mate(i)
        ag_copy(kbuf, t, z, k_sems).wait_send()
        ag_copy(vbuf, t, z, v_sems).wait_send()
        rs_copy(t, z, bufs_v, sems_v).wait_send()
        rs_copy(t, z, bufs_k, sems_k).wait_send()

    loop(Z - 1, drain)
    for cp in y_copies:
        cp.wait_send()


def on_device(Y, query_vectors, key_vectors, value_rows, forward_out, out_grad, block_offsets):
    T, QH, D = query_vectors.shape
    G = key_vectors.shape[1]
    H = QH // G
    N = lax.axis_size("ctx")
    Z = N // Y
    GL, C, HT, R = G // Y, Y * T, H * T, T * G
    Q = Y * HT
    vmem = pl.BlockSpec(memory_space=pltpu.VMEM)
    smem = pl.BlockSpec(memory_space=pltpu.SMEM)
    hbm = pl.BlockSpec(memory_space=pltpu.HBM)
    V = pltpu.VMEM
    part = V((GL * C, D), F32)
    wire = V((Z, GL * C, D), BF16)
    dq, dk, dv = pl.pallas_call(
        functools.partial(kernel, Z, Y, G, H, T, D),
        out_shape=(
            jax.ShapeDtypeStruct((T * QH, D), F32),
            jax.ShapeDtypeStruct((R, D), F32),
            jax.ShapeDtypeStruct((R, D), F32),
        ),
        in_specs=[hbm] * 5 + [smem],
        out_specs=[vmem] * 3,
        scratch_shapes=[
            V((T * QH, D), BF16), V((R, D), BF16), V((R, D), BF16),
            V((T * QH, D), BF16), V((T * QH, D), BF16), pltpu.SemaphoreType.DMA((5,)),
            V((T * QH, D), F32),
            V((GL, Q, D), BF16), V((GL, Q, D), BF16),
            V((GL, HT, D), BF16), V((GL, HT, D), BF16),
            V((GL, T + PAD, D), BF16), V((GL, T, D), BF16),
            V((GL, 1, Q), F32), V((GL, 1, HT), F32),
            V((Z, GL, Y * (T + PAD), D), BF16), V((Z, GL, C, D), BF16),
            V((GL, N * T, Q), F32), V((GL, N * T, Q), BF16), V((GL, 8, Q), F32),
            part, part, wire, wire, wire, wire,
            V((GL, HT, D), BF16), V((GL, HT, D), BF16),
            V((2, GL, T, D), BF16), V((2, GL, T, D), BF16),
            pltpu.SemaphoreType.DMA((8,)), pltpu.SemaphoreType.DMA((8,)),
        ] + [pltpu.SemaphoreType.DMA((Z,))] * 8,
        compiler_params=pltpu.CompilerParams(
            collective_id=0, has_side_effects=True, vmem_limit_bytes=56 * 1024 * 1024
        ),
        cost_estimate=pl.CostEstimate(
            flops=10 * GL * Q * N * T * D, bytes_accessed=4 * T * QH * D * 4,
            transcendentals=GL * Q * N * T,
        ),
    )(
        query_vectors.reshape(T * QH, D), key_vectors.reshape(R, D), value_rows.reshape(R, D),
        forward_out.reshape(T * QH, D), out_grad.reshape(T * QH, D), block_offsets,
    )
    return dq.reshape(T, QH, D), dk.reshape(T, G, D), dv.reshape(T, G, D)


def solution(mesh):
    pair = 2 if mesh.shape["groups"] == 2 and mesh.shape["ctx"] % 2 == 0 else 1
    tokens = P(("groups", "ctx"), "heads", None)
    return jax.shard_map(
        functools.partial(on_device, pair), mesh=mesh,
        in_specs=(tokens,) * 5 + (P(("groups", "ctx")),),
        out_specs=(tokens,) * 3, check_vma=False,
    )
```

```python
import functools

import jax
import jax.numpy as jnp
from jax import lax
from jax.experimental import pallas as pl
from jax.experimental.pallas import tpu as pltpu
from jax.sharding import PartitionSpec as P

MESH = pl.DeviceIdType.MESH
LOG2E = 1.4426950408889634
F32 = jnp.float32
BF16 = jnp.bfloat16
PAD = 16


def dot_nt(a, b):
    return lax.dot_general(a, b, (((1,), (1,)), ((), ())), preferred_element_type=F32)


def dot_nn(a, b):
    return lax.dot_general(a, b, (((1,), (0,)), ((), ())), preferred_element_type=F32)


def loop(n, body):
    if n <= 4:
        for i in range(n):
            body(i)
    else:
        def step(i, carry):
            body(i)
            return carry
        lax.fori_loop(0, n, step, 0)


def kernel(Z, Y, G, H, T, D, *refs):
    (q_hbm, k_hbm, v_hbm, fo_hbm, do_hbm, off_ref, dq_ref, dk_ref, dv_ref,
     q_ref, k_ref, v_ref, fo_ref, do_ref, in_sem,
     tmp, qs, dos, qst, dost, kst, vst, delta, delst, kbuf, vbuf,
     s_scr, ds_scr, top_scr,
     gsv, grv, gsk, grk, ownv, ownk, midv, midk, viav, viak,
     dqst, dqr, ys, yr, viav_s, viav_r, viak_s, viak_r,
     ks_s, ks_r, vs_s, vs_r, gv_s, gv_r, gk_s, gk_r) = refs
    me = lax.axis_index("ctx")
    z, y = me // Y, me % Y
    other = 1 - y if Y == 2 else 0
    scale = D ** (-0.5)
    GL = G // Y
    C = Y * T
    CP = Y * (T + PAD)
    HT = H * T
    N = Z * Y
    Q = Y * HT
    first = y * GL
    theirs = other * GL

    def at(zz, yy):
        return {"ctx": zz * Y + yy}

    inputs = [(k_hbm, k_ref), (q_hbm, q_ref), (v_hbm, v_ref), (do_hbm, do_ref), (fo_hbm, fo_ref)]
    loads = [pltpu.make_async_copy(a, b, in_sem.at[i]) for i, (a, b) in enumerate(inputs)]
    for cp in loads:
        cp.start()

    barrier = pltpu.get_barrier_semaphore()

    for d in range(Z):
        for yy in ([y] if d else []) + ([other] if Y == 2 else []):
            pl.semaphore_signal(
                barrier, inc=1, device_id=at(lax.rem(z + d, Z), yy), device_id_type=MESH)

    def head(src, heads, h):
        return tmp[pl.ds(h, T, stride=heads), :]

    def aligned(x):
        return pl.multiple_of(x, 16)

    def ycopy(i, src, dst):
        return pltpu.make_async_remote_copy(
            src_ref=src, dst_ref=dst, send_sem=ys.at[i], recv_sem=yr.at[i],
            device_id=at(z, other), device_id_type=MESH)

    own_rows = pl.ds(aligned(y * HT), HT)
    own_keys = pl.ds(aligned(y * (T + PAD)), T + PAD)
    own_vals = pl.ds(aligned(y * T), T)
    own_lanes = pl.ds(pl.multiple_of(y * HT, 128), HT)
    y_copies = []
    if Y == 2:
        y_copies = [
            ycopy(0, kst, kbuf.at[z, :, own_keys]),
            ycopy(1, qst, qs.at[:, own_rows]),
            ycopy(2, vst, vbuf.at[z, :, own_vals]),
            ycopy(3, dost, dos.at[:, own_rows]),
            ycopy(4, delst, delta.at[:, :, own_lanes]),
            ycopy(5, dqst, dqr),
        ]

    def y_start(i):
        if Y == 2:
            y_copies[i].start()

    def y_wait(i):
        if Y == 2:
            y_copies[i].wait_recv()

    def mate(i, near=True):
        if not near:
            i = Z - 2 - i
        up = i + jnp.where(i >= z, 1, 0)
        v = Z - 1 - i
        return jnp.where(z < Z // 2, up, v - jnp.where(v <= z, 1, 0))

    def ag_copy(buf, t, block, sems):
        return pltpu.make_async_remote_copy(
            src_ref=buf.at[block], dst_ref=buf.at[block],
            send_sem=sems[0].at[t], recv_sem=sems[1].at[block],
            device_id=at(t, y), device_id_type=MESH)

    relayed = Z == 4
    middle = (z > 0) & (z < Z - 1)

    def ag_send(buf, sems):
        if not relayed:
            loop(Z - 1, lambda i: ag_copy(buf, mate(i), z, sems).start())
            return
        pl.when(middle)(lambda: ag_copy(buf, mate(2), z, sems).start())
        ag_copy(buf, mate(1), z, sems).start()
        ag_copy(buf, mate(0), z, sems).start()

    def ag_relay(buf, sems):
        return pltpu.make_async_remote_copy(
            src_ref=buf.at[mate(2)], dst_ref=buf.at[mate(2)],
            send_sem=sems[0].at[z], recv_sem=sems[1].at[mate(2)],
            device_id=at(Z - 1 - mate(2), y), device_id_type=MESH)

    def arrival(i):
        if not relayed or i == 0:
            return mate(i)
        return mate(jnp.where(middle, 3 - i, i))

    def ag_recv(buf, i, sems):
        ag_copy(buf, arrival(i), arrival(i), sems).wait_recv()
        if relayed and i == 1:
            pl.when(middle)(lambda: ag_relay(buf, sems).start())

    def ag_drain(buf, i, sems):
        if not relayed or i < 2:
            ag_copy(buf, mate(i), z, sems).wait_send()
            return
        pl.when(middle)(lambda: ag_copy(buf, mate(2), z, sems).wait_send())
        pl.when(middle)(lambda: ag_relay(buf, sems).wait_send())

    k_sems = (ks_s, ks_r)
    v_sems = (vs_s, vs_r)

    own_off = off_ref[0].astype(F32)
    off_rows = jnp.full((PAD, D), own_off, F32).astype(BF16)
    loads[0].wait()
    tmp[0:T * G, :] = k_ref[...].astype(F32)
    for i in range(GL):
        kbuf[z, i, pl.ds(aligned(y * (T + PAD)), T), :] = head(tmp, G, first + i).astype(BF16)
        kbuf[z, i, pl.ds(aligned(y * (T + PAD) + T), PAD), :] = off_rows
        if Y == 2:
            kst[i, 0:T, :] = head(tmp, G, theirs + i).astype(BF16)
            kst[i, T:T + PAD, :] = off_rows
    pl.semaphore_wait(barrier, N - 1)
    y_start(0)

    def split_queries(dst, stage):
        for i in range(GL):
            for h in range(H):
                if Y == 2:
                    stage[i, pl.ds(h * T, T), :] = head(tmp, G * H, (theirs + i) * H + h).astype(BF16)
                dst[i, pl.ds(aligned(y * HT + h * T), T), :] = (
                    head(tmp, G * H, (first + i) * H + h).astype(BF16))

    loads[1].wait()
    tmp[...] = q_ref[...].astype(F32)
    split_queries(qs, qst)
    y_start(1)
    y_wait(0)
    ag_send(kbuf, k_sems)

    loads[2].wait()
    tmp[0:T * G, :] = v_ref[...].astype(F32)
    for i in range(GL):
        vbuf[z, i, own_vals, :] = head(tmp, G, first + i).astype(BF16)
        if Y == 2:
            vst[i] = head(tmp, G, theirs + i).astype(BF16)
    y_start(2)
    loads[3].wait()
    tmp[...] = do_ref[...].astype(F32)
    split_queries(dos, dost)
    y_start(3)

    loads[4].wait()
    tmp[...] = do_ref[...].astype(F32) * fo_ref[...].astype(F32)
    for i in range(GL):
        for h in range(H):
            def lanes(g):
                return jnp.sum(head(tmp, G * H, g * H + h).T, axis=0, keepdims=True)
            delta[i, :, pl.ds(pl.multiple_of(y * HT + h * T, 128), T)] = lanes(first + i)
            if Y == 2:
                delst[i, :, pl.ds(h * T, T)] = lanes(theirs + i)
    y_start(4)

    def key_rows(c, g):
        return jnp.concatenate([kbuf[c, g, pl.ds(i * (T + PAD), T), :] for i in range(Y)], axis=0)

    def block_off(c, i):
        return kbuf[c, 0, pl.ds(i * (T + PAD) + T, PAD), :][0:1, :].astype(F32)

    lead = (lax.broadcasted_iota(jnp.int32, (T, Q), 0)
            - lax.broadcasted_iota(jnp.int32, (T, Q), 1) % T).astype(F32)
    top_scr[...] = jnp.full(top_scr.shape, -1e30, F32)
    y_wait(1)
    q_off = jnp.concatenate([block_off(z, i) for i in range(Y) for h in range(H)], axis=1)

    def scores(c):
        for g in range(GL):
            s = dot_nt(key_rows(c, g), qs[g]) * (scale * LOG2E)
            parts = []
            for i in range(Y):
                off = jnp.concatenate([block_off(c, i)] * (Q // D), axis=1)
                parts.append(jnp.where(lead <= (q_off - off) * T, s[i * T:(i + 1) * T], -1e30))
            s = jnp.concatenate(parts, axis=0)
            s_scr[g, pl.ds(pl.multiple_of(c * C, 128), C), :] = s
            top_scr[g] = jnp.maximum(top_scr[g], jnp.max(s.reshape(C // 8, 8, Q), axis=0))

    scores(z)
    y_wait(2)
    ag_send(vbuf, v_sems)

    def key_arrival(i):
        ag_recv(kbuf, i, k_sems)
        scores(arrival(i))

    loop(Z - 1, key_arrival)

    tops = [jnp.max(top_scr[g], axis=0, keepdims=True) for g in range(GL)]

    def total_step(c, sums):
        new = []
        for g in range(GL):
            rows = pl.ds(pl.multiple_of(c * C, 128), C)
            e = jnp.exp2(s_scr[g, rows, :] - tops[g])
            s_scr[g, rows, :] = e
            new.append(sums[g] + jnp.sum(e.reshape(C // 8, 8, Q), axis=0))
        return tuple(new)

    sums = lax.fori_loop(0, Z, total_step, tuple(jnp.zeros((8, Q), F32) for _ in range(GL)))
    inv = [1.0 / jnp.sum(t, axis=0, keepdims=True) for t in sums]

    y_wait(3)

    class Sums:
        def __init__(self, send, recv, own, mid, via, ss, rs, via_s, via_r):
            self.send, self.recv, self.own, self.mid, self.via = send, recv, own, mid, via
            self.ss, self.rs, self.via_s, self.via_r = ss, rs, via_s, via_r

        def copy(self, c, half):
            return pltpu.make_async_remote_copy(
                src_ref=self.send.at[c, half], dst_ref=self.recv.at[z, y],
                send_sem=self.ss.at[c, half], recv_sem=self.rs.at[z, y],
                device_id=at(c, half), device_id_type=MESH)

        def arrive(self, src_z, src_y):
            pltpu.make_async_remote_copy(
                src_ref=self.send.at[z, y], dst_ref=self.recv.at[src_z, src_y],
                send_sem=self.ss.at[z, y], recv_sem=self.rs.at[src_z, src_y],
                device_id=at(lax.rem(z + 1, Z), y), device_id_type=MESH).wait_recv()

        def to_middle(self):
            return pltpu.make_async_remote_copy(
                src_ref=self.send.at[mate(Z - 2)], dst_ref=self.via,
                send_sem=self.via_s, recv_sem=self.via_r,
                device_id=at(mate(0), y), device_id_type=MESH)

        def start(self, c):
            for half in range(Y):
                self.copy(c, half).start()

    sum_v = Sums(gsv, grv, ownv, midv, viav, gv_s, gv_r, viav_s, viav_r)
    sum_k = Sums(gsk, grk, ownk, midk, viak, gk_s, gk_r, viak_s, viak_r)

    def value_chunk(c, put):
        rows = pl.ds(pl.multiple_of(c * C, 128), C)
        for g in range(GL):
            p = s_scr[g, rows, :] * inv[g]
            s_scr[g, rows, :] = p
            put(g, dot_nn(p.astype(BF16), dos[g]))

    def key_chunk(c, put):
        rows = pl.ds(pl.multiple_of(c * C, 128), C)
        for g in range(GL):
            dp = dot_nt(vbuf[c, g], dos[g])
            ds = (s_scr[g, rows, :] * (dp - delta[g])).astype(BF16)
            ds_scr[g, rows, :] = ds
            put(g, dot_nn(ds, qs[g]) * scale)

    def putter(ref):
        def put(g, x):
            for half in range(Y):
                ref[half, pl.ds(g * T, T), :] = x[half * T:(half + 1) * T].astype(ref.dtype)
        return put

    def send_chunks(chunk, sums):
        if not relayed:
            def one(i):
                c = mate(i, False)
                chunk(c, putter(sums.send.at[c]))
                sums.start(c)
            loop(Z - 1, one)
            return

        @pl.when(jnp.logical_not(middle))
        def _():
            c = mate(2)
            chunk(c, putter(sums.send.at[c]))
            sums.to_middle().start()

        for i in (1, 0):
            c = mate(i)
            chunk(c, putter(sums.send.at[c]))
            sums.start(c)
        pl.when(middle)(lambda: chunk(mate(2), putter(sums.mid)))

    def own_chunk(chunk, sums):
        chunk(z, putter(sums.own))
        if Y == 2:
            sums.send[z, other] = sums.own[other].astype(BF16)
            sums.copy(z, other).start()

    def pass_on(sums):
        if relayed:
            @pl.when(middle)
            def _():
                c = mate(2)
                sums.to_middle().wait_recv()
                sums.send[c] = (sums.mid[...] + sums.via[...].astype(F32)).astype(BF16)
                sums.start(c)

    send_chunks(value_chunk, sum_v)
    own_chunk(value_chunk, sum_v)
    y_wait(4)
    ag_recv(vbuf, 0, v_sems)
    if Z > 2:
        ag_recv(vbuf, 1, v_sems)
    pass_on(sum_v)
    loop(Z - 3, lambda i: ag_recv(vbuf, i + 2, v_sems))
    send_chunks(key_chunk, sum_k)
    own_chunk(key_chunk, sum_k)
    pass_on(sum_k)

    for g in range(GL):
        kt = jnp.concatenate(
            [key_rows(c, g).astype(F32).T.astype(BF16) for c in range(Z)], axis=1)
        dqt = dot_nn(kt, ds_scr[g]) * scale
        for i in range(Y):
            for h in range(H):
                block = dqt[:, (i * H + h) * T:(i * H + h + 1) * T].T

                def keep(block=block, h=h):
                    dq_ref[pl.ds((first + g) * H + h, T, stride=G * H), :] = block

                def stage(block=block, h=h):
                    dqst[g, pl.ds(h * T, T), :] = block.astype(BF16)

                if Y == 2:
                    pl.when(y == i)(keep)
                    pl.when(y != i)(stage)
                else:
                    keep()
    y_start(5)

    def finish(out, sums):
        def add_from(src):
            sums.arrive(src, y)
            sums.own[y] = sums.own[y] + sums.recv[src, y].astype(F32)
            if Y == 2:
                sums.arrive(src, other)
                sums.own[other] = sums.own[other] + sums.recv[src, other].astype(F32)

        def add(i):
            if relayed and i == 2:
                pl.when(middle)(lambda: add_from(mate(i)))
            else:
                add_from(mate(i))

        if Y == 2:
            sums.arrive(z, other)
            sums.own[other] = sums.recv[z, other].astype(F32)
        loop(Z - 1, add)
        for g in range(GL):
            out[pl.ds(first + g, T, stride=G), :] = sums.own[y, pl.ds(g * T, T), :]
            if Y == 2:
                out[pl.ds(theirs + g, T, stride=G), :] = sums.own[other, pl.ds(g * T, T), :]

    finish(dv_ref, sum_v)
    y_wait(5)
    if Y == 2:
        for g in range(GL):
            for h in range(H):
                dq_ref[pl.ds((theirs + g) * H + h, T, stride=G * H), :] = (
                    dqr[g, pl.ds(h * T, T), :].astype(F32))
    finish(dk_ref, sum_k)

    def drain(i):
        ag_drain(kbuf, i, k_sems)
        ag_drain(vbuf, i, v_sems)
        for sums in (sum_v, sum_k):
            def direct(sums=sums):
                for half in range(Y):
                    sums.copy(mate(i), half).wait_send()

            if relayed and i == 2:
                pl.when(middle)(direct)
                pl.when(jnp.logical_not(middle))(sums.to_middle().wait_send)
            else:
                direct()

    loop(Z - 1, drain)
    if Y == 2:
        sum_v.copy(z, other).wait_send()
        sum_k.copy(z, other).wait_send()
    for cp in y_copies:
        cp.wait_send()


def on_device(Y, query_vectors, key_vectors, value_rows, forward_out, out_grad, block_offsets):
    T, QH, D = query_vectors.shape
    G = key_vectors.shape[1]
    H = QH // G
    N = lax.axis_size("ctx")
    Z = N // Y
    GL, C, HT, R = G // Y, Y * T, H * T, T * G
    Q = Y * HT
    vmem = pl.BlockSpec(memory_space=pltpu.VMEM)
    smem = pl.BlockSpec(memory_space=pltpu.SMEM)
    hbm = pl.BlockSpec(memory_space=pltpu.HBM)
    V = pltpu.VMEM
    own = V((Y, GL * T, D), F32)
    wire = V((Z, Y, GL * T, D), BF16)
    dq, dk, dv = pl.pallas_call(
        functools.partial(kernel, Z, Y, G, H, T, D),
        out_shape=(
            jax.ShapeDtypeStruct((T * QH, D), F32),
            jax.ShapeDtypeStruct((R, D), F32),
            jax.ShapeDtypeStruct((R, D), F32),
        ),
        in_specs=[hbm] * 5 + [smem],
        out_specs=[vmem] * 3,
        scratch_shapes=[
            V((T * QH, D), BF16), V((R, D), BF16), V((R, D), BF16),
            V((T * QH, D), BF16), V((T * QH, D), BF16), pltpu.SemaphoreType.DMA((5,)),
            V((T * QH, D), F32),
            V((GL, Q, D), BF16), V((GL, Q, D), BF16),
            V((GL, HT, D), BF16), V((GL, HT, D), BF16),
            V((GL, T + PAD, D), BF16), V((GL, T, D), BF16),
            V((GL, 1, Q), F32), V((GL, 1, HT), F32),
            V((Z, GL, Y * (T + PAD), D), BF16), V((Z, GL, C, D), BF16),
            V((GL, N * T, Q), F32), V((GL, N * T, Q), BF16), V((GL, 8, Q), F32),
            wire, wire, wire, wire, own, own, own, own, V((Y, GL * T, D), BF16), V((Y, GL * T, D), BF16),
            V((GL, HT, D), BF16), V((GL, HT, D), BF16),
            pltpu.SemaphoreType.DMA((6,)), pltpu.SemaphoreType.DMA((6,)),
        ] + [pltpu.SemaphoreType.DMA] * 4 + [pltpu.SemaphoreType.DMA((Z,))] * 4
        + [pltpu.SemaphoreType.DMA((Z, Y))] * 4,
        compiler_params=pltpu.CompilerParams(
            collective_id=0, has_side_effects=True, vmem_limit_bytes=56 * 1024 * 1024
        ),
        cost_estimate=pl.CostEstimate(
            flops=10 * GL * Q * N * T * D, bytes_accessed=4 * T * QH * D * 4,
            transcendentals=GL * Q * N * T,
        ),
    )(
        query_vectors.reshape(T * QH, D), key_vectors.reshape(R, D), value_rows.reshape(R, D),
        forward_out.reshape(T * QH, D), out_grad.reshape(T * QH, D), block_offsets,
    )
    return dq.reshape(T, QH, D), dk.reshape(T, G, D), dv.reshape(T, G, D)


def solution(mesh):
    pair = 2 if mesh.shape["groups"] == 2 and mesh.shape["ctx"] % 2 == 0 else 1
    tokens = P(("groups", "ctx"), "heads", None)
    return jax.shard_map(
        functools.partial(on_device, pair), mesh=mesh,
        in_specs=(tokens,) * 5 + (P(("groups", "ctx")),),
        out_specs=(tokens,) * 3, check_vma=False,
    )
```

```python
import functools

import jax
import jax.numpy as jnp
from jax import lax
from jax.experimental import pallas as pl
from jax.experimental.pallas import tpu as pltpu
from jax.sharding import PartitionSpec as P

MESH = pl.DeviceIdType.MESH
LOG2E = 1.4426950408889634
F32 = jnp.float32
BF16 = jnp.bfloat16
PAD = 16


def dot_nt(a, b):
    return lax.dot_general(a, b, (((1,), (1,)), ((), ())), preferred_element_type=F32)


def dot_nn(a, b):
    return lax.dot_general(a, b, (((1,), (0,)), ((), ())), preferred_element_type=F32)


def loop(n, body):
    if n <= 4:
        for i in range(n):
            body(i)
    else:
        def step(i, carry):
            body(i)
            return carry
        lax.fori_loop(0, n, step, 0)


def kernel(Z, Y, G, H, T, D, *refs):
    (q_hbm, k_hbm, v_hbm, fo_hbm, do_hbm, off_ref, dq_ref, dk_ref, dv_ref,
     q_ref, k_ref, v_ref, fo_ref, do_ref, in_sem,
     tmp, qs, dos, qst, dost, kst, vst, delta, delst, kbuf, vbuf,
     s_scr, ds_scr, top_scr,
     gsv, grv, gsk, grk, ownv, ownk, midv, midk, viav, viak,
     dqst, dqr, ys, yr, viav_s, viav_r, viak_s, viak_r,
     ks_s, ks_r, vs_s, vs_r, gv_s, gv_r, gk_s, gk_r) = refs
    me = lax.axis_index("ctx")
    z, y = me // Y, me % Y
    other = 1 - y if Y == 2 else 0
    scale = D ** (-0.5)
    GL = G // Y
    C = Y * T
    CP = Y * (T + PAD)
    HT = H * T
    N = Z * Y
    Q = Y * HT
    first = y * GL
    theirs = other * GL

    def at(zz, yy):
        return {"ctx": zz * Y + yy}

    inputs = [(k_hbm, k_ref), (q_hbm, q_ref), (v_hbm, v_ref), (do_hbm, do_ref), (fo_hbm, fo_ref)]
    loads = [pltpu.make_async_copy(a, b, in_sem.at[i]) for i, (a, b) in enumerate(inputs)]
    for cp in loads:
        cp.start()

    barrier = pltpu.get_barrier_semaphore()

    for d in range(Z):
        for yy in ([y] if d else []) + ([other] if Y == 2 else []):
            pl.semaphore_signal(
                barrier, inc=1, device_id=at(lax.rem(z + d, Z), yy), device_id_type=MESH)

    def head(src, heads, h):
        return tmp[pl.ds(h, T, stride=heads), :]

    def aligned(x):
        return pl.multiple_of(x, 16)

    def ycopy(i, src, dst):
        return pltpu.make_async_remote_copy(
            src_ref=src, dst_ref=dst, send_sem=ys.at[i], recv_sem=yr.at[i],
            device_id=at(z, other), device_id_type=MESH)

    own_rows = pl.ds(aligned(y * HT), HT)
    own_keys = pl.ds(aligned(y * (T + PAD)), T + PAD)
    own_vals = pl.ds(aligned(y * T), T)
    own_lanes = pl.ds(pl.multiple_of(y * HT, 128), HT)
    y_copies = []
    if Y == 2:
        y_copies = [
            ycopy(0, qst, qs.at[:, own_rows]),
            ycopy(1, vst, vbuf.at[z, :, own_vals]),
            ycopy(2, dost, dos.at[:, own_rows]),
            ycopy(3, delst, delta.at[:, :, own_lanes]),
            ycopy(4, dqst, dqr),
        ]

    def y_start(i):
        if Y == 2:
            y_copies[i].start()

    def y_wait(i):
        if Y == 2:
            y_copies[i].wait_recv()

    def mate(i, near=True):
        if not near:
            i = Z - 2 - i
        up = i + jnp.where(i >= z, 1, 0)
        v = Z - 1 - i
        return jnp.where(z < Z // 2, up, v - jnp.where(v <= z, 1, 0))

    def ag_copy(buf, t, block, sems):
        return pltpu.make_async_remote_copy(
            src_ref=buf.at[block], dst_ref=buf.at[block],
            send_sem=sems[0].at[t], recv_sem=sems[1].at[block],
            device_id=at(t, y), device_id_type=MESH)

    middle = (z > 0) & (z < Z - 1)

    def ag_send(buf, sems):
        loop(Z - 1, lambda i: ag_copy(buf, mate(i), z, sems).start())

    def ag_recv(buf, i, sems):
        ag_copy(buf, mate(i), mate(i), sems).wait_recv()

    def key_copy(t, half):
        dst = kbuf.at[z, :, own_keys]
        return pltpu.make_async_remote_copy(
            src_ref=dst if half == 0 else kst, dst_ref=dst,
            send_sem=ks_s.at[t, half], recv_sem=ks_r.at[z, y],
            device_id=at(t, y if half == 0 else other), device_id_type=MESH)

    def key_wait(c, yy):
        pltpu.make_async_remote_copy(
            src_ref=kst, dst_ref=kbuf.at[c, :, pl.ds(aligned(yy * (T + PAD)), T + PAD)],
            send_sem=ks_s.at[z, 0], recv_sem=ks_r.at[c, yy],
            device_id=at(lax.rem(z + 1, Z), y), device_id_type=MESH).wait_recv()

    def key_send():
        if Y == 2:
            key_copy(z, 1).start()

        def one(i):
            for half in range(Y):
                key_copy(mate(i), half).start()

        loop(Z - 1, one)

    def key_recv(c):
        for yy in ([y] if Y == 1 else [y, other]):
            key_wait(c, yy)

    def key_drain(i):
        for half in range(Y):
            key_copy(mate(i), half).wait_send()

    v_sems = (vs_s, vs_r)

    own_off = off_ref[0].astype(F32)
    off_rows = jnp.full((PAD, D), own_off, F32).astype(BF16)
    loads[0].wait()
    tmp[0:T * G, :] = k_ref[...].astype(F32)
    for i in range(GL):
        kbuf[z, i, pl.ds(aligned(y * (T + PAD)), T), :] = head(tmp, G, first + i).astype(BF16)
        kbuf[z, i, pl.ds(aligned(y * (T + PAD) + T), PAD), :] = off_rows
        if Y == 2:
            kst[i, 0:T, :] = head(tmp, G, theirs + i).astype(BF16)
            kst[i, T:T + PAD, :] = off_rows
    pl.semaphore_wait(barrier, N - 1)
    key_send()

    def split_queries(dst, stage):
        for i in range(GL):
            for h in range(H):
                if Y == 2:
                    stage[i, pl.ds(h * T, T), :] = head(tmp, G * H, (theirs + i) * H + h).astype(BF16)
                dst[i, pl.ds(aligned(y * HT + h * T), T), :] = (
                    head(tmp, G * H, (first + i) * H + h).astype(BF16))

    loads[1].wait()
    tmp[...] = q_ref[...].astype(F32)
    split_queries(qs, qst)
    y_start(0)

    loads[2].wait()
    tmp[0:T * G, :] = v_ref[...].astype(F32)
    for i in range(GL):
        vbuf[z, i, own_vals, :] = head(tmp, G, first + i).astype(BF16)
        if Y == 2:
            vst[i] = head(tmp, G, theirs + i).astype(BF16)
    y_start(1)
    loads[3].wait()
    tmp[...] = do_ref[...].astype(F32)
    split_queries(dos, dost)
    y_start(2)

    loads[4].wait()
    tmp[...] = do_ref[...].astype(F32) * fo_ref[...].astype(F32)
    for i in range(GL):
        for h in range(H):
            def lanes(g):
                return jnp.sum(head(tmp, G * H, g * H + h).T, axis=0, keepdims=True)
            delta[i, :, pl.ds(pl.multiple_of(y * HT + h * T, 128), T)] = lanes(first + i)
            if Y == 2:
                delst[i, :, pl.ds(h * T, T)] = lanes(theirs + i)
    y_start(3)

    def key_rows(c, g):
        return jnp.concatenate([kbuf[c, g, pl.ds(i * (T + PAD), T), :] for i in range(Y)], axis=0)

    def block_off(c, i):
        return kbuf[c, 0, pl.ds(i * (T + PAD) + T, PAD), :][0:1, :].astype(F32)

    lead = (lax.broadcasted_iota(jnp.int32, (T, Q), 0)
            - lax.broadcasted_iota(jnp.int32, (T, Q), 1) % T).astype(F32)
    top_scr[...] = jnp.full(top_scr.shape, -1e30, F32)
    y_wait(0)
    if Y == 2:
        key_wait(z, other)
    q_off = jnp.concatenate([block_off(z, i) for i in range(Y) for h in range(H)], axis=1)

    def scores(c):
        for g in range(GL):
            s = dot_nt(key_rows(c, g), qs[g]) * (scale * LOG2E)
            parts = []
            for i in range(Y):
                off = jnp.concatenate([block_off(c, i)] * (Q // D), axis=1)
                parts.append(jnp.where(lead <= (q_off - off) * T, s[i * T:(i + 1) * T], -1e30))
            s = jnp.concatenate(parts, axis=0)
            s_scr[g, pl.ds(pl.multiple_of(c * C, 128), C), :] = s
            top_scr[g] = jnp.maximum(top_scr[g], jnp.max(s.reshape(C // 8, 8, Q), axis=0))

    scores(z)
    y_wait(1)
    ag_send(vbuf, v_sems)

    def key_arrival(i):
        key_recv(mate(i))
        scores(mate(i))

    loop(Z - 1, key_arrival)

    tops = [jnp.max(top_scr[g], axis=0, keepdims=True) for g in range(GL)]

    def total_step(c, sums):
        new = []
        for g in range(GL):
            rows = pl.ds(pl.multiple_of(c * C, 128), C)
            e = jnp.exp2(s_scr[g, rows, :] - tops[g])
            s_scr[g, rows, :] = e
            new.append(sums[g] + jnp.sum(e.reshape(C // 8, 8, Q), axis=0))
        return tuple(new)

    sums = lax.fori_loop(0, Z, total_step, tuple(jnp.zeros((8, Q), F32) for _ in range(GL)))
    inv = [1.0 / jnp.sum(t, axis=0, keepdims=True) for t in sums]

    y_wait(2)

    class Sums:
        def __init__(self, relayed, send, recv, own, mid, via, ss, rs, via_s, via_r):
            self.relayed = relayed and Z == 4
            self.send, self.recv, self.own, self.mid, self.via = send, recv, own, mid, via
            self.ss, self.rs, self.via_s, self.via_r = ss, rs, via_s, via_r

        def copy(self, c, half):
            return pltpu.make_async_remote_copy(
                src_ref=self.send.at[c, half], dst_ref=self.recv.at[z, y],
                send_sem=self.ss.at[c, half], recv_sem=self.rs.at[z, y],
                device_id=at(c, half), device_id_type=MESH)

        def arrive(self, src_z, src_y):
            pltpu.make_async_remote_copy(
                src_ref=self.send.at[z, y], dst_ref=self.recv.at[src_z, src_y],
                send_sem=self.ss.at[z, y], recv_sem=self.rs.at[src_z, src_y],
                device_id=at(lax.rem(z + 1, Z), y), device_id_type=MESH).wait_recv()

        def to_middle(self):
            return pltpu.make_async_remote_copy(
                src_ref=self.send.at[mate(Z - 2)], dst_ref=self.via,
                send_sem=self.via_s, recv_sem=self.via_r,
                device_id=at(mate(0), y), device_id_type=MESH)

        def start(self, c):
            for half in range(Y):
                self.copy(c, half).start()

    sum_v = Sums(True, gsv, grv, ownv, midv, viav, gv_s, gv_r, viav_s, viav_r)
    sum_k = Sums(False, gsk, grk, ownk, midk, viak, gk_s, gk_r, viak_s, viak_r)

    def value_chunk(c, put):
        rows = pl.ds(pl.multiple_of(c * C, 128), C)
        for g in range(GL):
            p = s_scr[g, rows, :] * inv[g]
            s_scr[g, rows, :] = p
            put(g, dot_nn(p.astype(BF16), dos[g]))

    def key_chunk(c, put):
        rows = pl.ds(pl.multiple_of(c * C, 128), C)
        for g in range(GL):
            dp = dot_nt(vbuf[c, g], dos[g])
            ds = (s_scr[g, rows, :] * (dp - delta[g])).astype(BF16)
            ds_scr[g, rows, :] = ds
            put(g, dot_nn(ds, qs[g]) * scale)

    def putter(ref):
        def put(g, x):
            for half in range(Y):
                ref[half, pl.ds(g * T, T), :] = x[half * T:(half + 1) * T].astype(ref.dtype)
        return put

    def send_chunks(chunk, sums):
        if not sums.relayed:
            def one(i):
                c = mate(i, False)
                chunk(c, putter(sums.send.at[c]))
                sums.start(c)
            loop(Z - 1, one)
            return

        @pl.when(jnp.logical_not(middle))
        def _():
            c = mate(2)
            chunk(c, putter(sums.send.at[c]))
            sums.to_middle().start()

        for i in (1, 0):
            c = mate(i)
            chunk(c, putter(sums.send.at[c]))
            sums.start(c)
        pl.when(middle)(lambda: chunk(mate(2), putter(sums.mid)))

    def own_chunk(chunk, sums):
        chunk(z, putter(sums.own))
        if Y == 2:
            sums.send[z, other] = sums.own[other].astype(BF16)
            sums.copy(z, other).start()

    def pass_on(sums):
        if sums.relayed:
            @pl.when(middle)
            def _():
                c = mate(2)
                sums.to_middle().wait_recv()
                sums.send[c] = (sums.mid[...] + sums.via[...].astype(F32)).astype(BF16)
                sums.start(c)

    send_chunks(value_chunk, sum_v)
    own_chunk(value_chunk, sum_v)
    y_wait(3)
    loop(Z - 1, lambda i: ag_recv(vbuf, i, v_sems))
    send_chunks(key_chunk, sum_k)
    pass_on(sum_v)
    own_chunk(key_chunk, sum_k)

    for g in range(GL):
        kt = jnp.concatenate(
            [key_rows(c, g).astype(F32).T.astype(BF16) for c in range(Z)], axis=1)
        dqt = dot_nn(kt, ds_scr[g]) * scale
        for i in range(Y):
            for h in range(H):
                block = dqt[:, (i * H + h) * T:(i * H + h + 1) * T].T

                def keep(block=block, h=h):
                    dq_ref[pl.ds((first + g) * H + h, T, stride=G * H), :] = block

                def stage(block=block, h=h):
                    dqst[g, pl.ds(h * T, T), :] = block.astype(BF16)

                if Y == 2:
                    pl.when(y == i)(keep)
                    pl.when(y != i)(stage)
                else:
                    keep()
    y_start(4)

    def finish(out, sums):
        def add_from(src):
            sums.arrive(src, y)
            sums.own[y] = sums.own[y] + sums.recv[src, y].astype(F32)
            if Y == 2:
                sums.arrive(src, other)
                sums.own[other] = sums.own[other] + sums.recv[src, other].astype(F32)

        def add(i):
            if sums.relayed and i == 2:
                pl.when(middle)(lambda: add_from(mate(i)))
            else:
                add_from(mate(i))

        if Y == 2:
            sums.arrive(z, other)
            sums.own[other] = sums.recv[z, other].astype(F32)
        loop(Z - 1, add)
        for g in range(GL):
            out[pl.ds(first + g, T, stride=G), :] = sums.own[y, pl.ds(g * T, T), :]
            if Y == 2:
                out[pl.ds(theirs + g, T, stride=G), :] = sums.own[other, pl.ds(g * T, T), :]

    finish(dv_ref, sum_v)
    y_wait(4)
    if Y == 2:
        for g in range(GL):
            for h in range(H):
                dq_ref[pl.ds((theirs + g) * H + h, T, stride=G * H), :] = (
                    dqr[g, pl.ds(h * T, T), :].astype(F32))
    finish(dk_ref, sum_k)

    def drain(i):
        key_drain(i)
        ag_copy(vbuf, mate(i), z, v_sems).wait_send()
        for sums in (sum_v, sum_k):
            def direct(sums=sums):
                for half in range(Y):
                    sums.copy(mate(i), half).wait_send()

            if sums.relayed and i == 2:
                pl.when(middle)(direct)
                pl.when(jnp.logical_not(middle))(sums.to_middle().wait_send)
            else:
                direct()

    loop(Z - 1, drain)
    if Y == 2:
        key_copy(z, 1).wait_send()
        sum_v.copy(z, other).wait_send()
        sum_k.copy(z, other).wait_send()
    for cp in y_copies:
        cp.wait_send()


def hand_over(a_ref, b_ref, c_ref, a_out, b_out, c_out, sem):
    copies = [
        pltpu.make_async_copy(src, dst, sem.at[i])
        for i, (src, dst) in enumerate([(a_ref, a_out), (b_ref, b_out), (c_ref, c_out)])
    ]
    for cp in copies:
        cp.start()
    for cp in copies:
        cp.wait()


def on_device(Y, query_vectors, key_vectors, value_rows, forward_out, out_grad, block_offsets):
    T, QH, D = query_vectors.shape
    G = key_vectors.shape[1]
    H = QH // G
    N = lax.axis_size("ctx")
    Z = N // Y
    GL, C, HT, R = G // Y, Y * T, H * T, T * G
    Q = Y * HT
    vmem = pl.BlockSpec(memory_space=pltpu.VMEM)
    smem = pl.BlockSpec(memory_space=pltpu.SMEM)
    hbm = pl.BlockSpec(memory_space=pltpu.HBM)
    V = pltpu.VMEM
    own = V((Y, GL * T, D), F32)
    wire = V((Z, Y, GL * T, D), BF16)
    dq, dk, dv = pl.pallas_call(
        functools.partial(kernel, Z, Y, G, H, T, D),
        out_shape=(
            jax.ShapeDtypeStruct((T * QH, D), F32),
            jax.ShapeDtypeStruct((R, D), F32),
            jax.ShapeDtypeStruct((R, D), F32),
        ),
        in_specs=[hbm] * 5 + [smem],
        out_specs=[vmem] * 3,
        scratch_shapes=[
            V((T * QH, D), BF16), V((R, D), BF16), V((R, D), BF16),
            V((T * QH, D), BF16), V((T * QH, D), BF16), pltpu.SemaphoreType.DMA((5,)),
            V((T * QH, D), F32),
            V((GL, Q, D), BF16), V((GL, Q, D), BF16),
            V((GL, HT, D), BF16), V((GL, HT, D), BF16),
            V((GL, T + PAD, D), BF16), V((GL, T, D), BF16),
            V((GL, 1, Q), F32), V((GL, 1, HT), F32),
            V((Z, GL, Y * (T + PAD), D), BF16), V((Z, GL, C, D), BF16),
            V((GL, N * T, Q), F32), V((GL, N * T, Q), BF16), V((GL, 8, Q), F32),
            wire, wire, wire, wire, own, own, own, own, V((Y, GL * T, D), BF16), V((Y, GL * T, D), BF16),
            V((GL, HT, D), BF16), V((GL, HT, D), BF16),
            pltpu.SemaphoreType.DMA((5,)), pltpu.SemaphoreType.DMA((5,)),
        ] + [pltpu.SemaphoreType.DMA] * 4 + [pltpu.SemaphoreType.DMA((Z, Y))] * 2
        + [pltpu.SemaphoreType.DMA((Z,))] * 2 + [pltpu.SemaphoreType.DMA((Z, Y))] * 4,
        compiler_params=pltpu.CompilerParams(
            collective_id=0, has_side_effects=True, vmem_limit_bytes=56 * 1024 * 1024
        ),
        cost_estimate=pl.CostEstimate(
            flops=10 * GL * Q * N * T * D, bytes_accessed=4 * T * QH * D * 4,
            transcendentals=GL * Q * N * T,
        ),
    )(
        query_vectors.reshape(T * QH, D), key_vectors.reshape(R, D), value_rows.reshape(R, D),
        forward_out.reshape(T * QH, D), out_grad.reshape(T * QH, D), block_offsets,
    )
    dq, dk, dv = pl.pallas_call(
        hand_over,
        out_shape=[jax.ShapeDtypeStruct(x.shape, x.dtype) for x in (dq, dk, dv)],
        in_specs=[hbm] * 3,
        out_specs=[hbm] * 3,
        scratch_shapes=[pltpu.SemaphoreType.DMA((3,))],
        compiler_params=pltpu.CompilerParams(vmem_limit_bytes=56 * 1024 * 1024),
        cost_estimate=pl.CostEstimate(
            flops=0, bytes_accessed=8 * (T * QH + 2 * R) * D, transcendentals=0),
    )(dq, dk, dv)
    return dq.reshape(T, QH, D), dk.reshape(T, G, D), dv.reshape(T, G, D)


def solution(mesh):
    pair = 2 if mesh.shape["groups"] == 2 and mesh.shape["ctx"] % 2 == 0 else 1
    tokens = P(("groups", "ctx"), "heads", None)
    return jax.shard_map(
        functools.partial(on_device, pair), mesh=mesh,
        in_specs=(tokens,) * 5 + (P(("groups", "ctx")),),
        out_specs=(tokens,) * 3, check_vma=False,
    )
```

```python
import functools

import jax
import jax.numpy as jnp
from jax import lax
from jax.experimental import pallas as pl
from jax.experimental.pallas import tpu as pltpu
from jax.sharding import PartitionSpec as P

MESH = pl.DeviceIdType.MESH
LOG2E = 1.4426950408889634
F32 = jnp.float32
BF16 = jnp.bfloat16
PAD = 16


def dot_nt(a, b):
    return lax.dot_general(a, b, (((1,), (1,)), ((), ())), preferred_element_type=F32)


def dot_nn(a, b):
    return lax.dot_general(a, b, (((1,), (0,)), ((), ())), preferred_element_type=F32)


def loop(n, body):
    if n <= 4:
        for i in range(n):
            body(i)
    else:
        def step(i, carry):
            body(i)
            return carry
        lax.fori_loop(0, n, step, 0)


def kernel(Z, Y, G, H, T, D, *refs):
    (q_hbm, k_hbm, v_hbm, fo_hbm, do_hbm, off_ref, dq_ref, dk_ref, dv_ref,
     q_ref, k_ref, v_ref, fo_ref, do_ref, in_sem,
     tmp, qs, dos, qst, dost, kst, vst, delta, delst, kbuf, vbuf,
     s_scr, ds_scr, top_scr,
     gsv, grv, gsk, grk, ownv, ownk, midv, midk, viav, viak,
     dqst, dqr, ys, yr, viav_s, viav_r, viak_s, viak_r,
     ks_s, ks_r, vs_s, vs_r, gv_s, gv_r, gk_s, gk_r) = refs
    me = lax.axis_index("ctx")
    z, y = me // Y, me % Y
    other = 1 - y if Y == 2 else 0
    scale = D ** (-0.5)
    GL = G // Y
    C = Y * T
    CP = Y * (T + PAD)
    HT = H * T
    N = Z * Y
    Q = Y * HT
    first = y * GL
    theirs = other * GL

    def at(zz, yy):
        return {"ctx": zz * Y + yy}

    inputs = [(k_hbm, k_ref), (q_hbm, q_ref), (v_hbm, v_ref), (do_hbm, do_ref), (fo_hbm, fo_ref)]
    loads = [pltpu.make_async_copy(a, b, in_sem.at[i]) for i, (a, b) in enumerate(inputs)]
    for cp in loads:
        cp.start()

    barrier = pltpu.get_barrier_semaphore()

    for d in range(Z):
        for yy in ([y] if d else []) + ([other] if Y == 2 else []):
            pl.semaphore_signal(
                barrier, inc=1, device_id=at(lax.rem(z + d, Z), yy), device_id_type=MESH)

    def head(src, heads, h):
        return tmp[pl.ds(h, T, stride=heads), :]

    def aligned(x):
        return pl.multiple_of(x, 16)

    def ycopy(i, src, dst):
        return pltpu.make_async_remote_copy(
            src_ref=src, dst_ref=dst, send_sem=ys.at[i], recv_sem=yr.at[i],
            device_id=at(z, other), device_id_type=MESH)

    own_rows = pl.ds(aligned(y * HT), HT)
    own_keys = pl.ds(aligned(y * (T + PAD)), T + PAD)
    own_vals = pl.ds(aligned(y * T), T)
    own_lanes = pl.ds(pl.multiple_of(y * HT, 128), HT)
    y_copies = []
    if Y == 2:
        y_copies = [
            ycopy(0, qst, qs.at[:, own_rows]),
            ycopy(1, vst, vbuf.at[z, :, own_vals]),
            ycopy(2, dost, dos.at[:, own_rows]),
            ycopy(3, delst, delta.at[:, :, own_lanes]),
            ycopy(4, dqst, dqr),
        ]

    def y_start(i):
        if Y == 2:
            y_copies[i].start()

    def y_wait(i):
        if Y == 2:
            y_copies[i].wait_recv()

    def mate(i, near=True):
        if not near:
            i = Z - 2 - i
        up = i + jnp.where(i >= z, 1, 0)
        v = Z - 1 - i
        return jnp.where(z < Z // 2, up, v - jnp.where(v <= z, 1, 0))

    def ag_copy(buf, t, block, sems):
        return pltpu.make_async_remote_copy(
            src_ref=buf.at[block], dst_ref=buf.at[block],
            send_sem=sems[0].at[t], recv_sem=sems[1].at[block],
            device_id=at(t, y), device_id_type=MESH)

    middle = (z > 0) & (z < Z - 1)

    relayed = Z == 4

    def ag_send(buf, sems):
        if not relayed:
            loop(Z - 1, lambda i: ag_copy(buf, mate(i), z, sems).start())
            return
        ag_copy(buf, mate(1), z, sems).start()
        ag_copy(buf, mate(0), z, sems).start()
        pl.when(middle)(lambda: ag_copy(buf, mate(2), z, sems).start())

    def ag_relay(buf, sems):
        return pltpu.make_async_remote_copy(
            src_ref=buf.at[mate(2)], dst_ref=buf.at[mate(2)],
            send_sem=sems[0].at[z], recv_sem=sems[1].at[mate(2)],
            device_id=at(Z - 1 - mate(2), y), device_id_type=MESH)

    def arrival(i):
        if not relayed or i == 0:
            return mate(i)
        return mate(jnp.where(middle, 3 - i, i))

    def ag_recv(buf, i, sems):
        ag_copy(buf, arrival(i), arrival(i), sems).wait_recv()
        if relayed and i == 1:
            pl.when(middle)(lambda: ag_relay(buf, sems).start())

    def ag_drain(buf, i, sems):
        if not relayed or i < 2:
            ag_copy(buf, mate(i), z, sems).wait_send()
            return
        pl.when(middle)(lambda: ag_copy(buf, mate(2), z, sems).wait_send())
        pl.when(middle)(lambda: ag_relay(buf, sems).wait_send())

    def key_copy(t, half):
        dst = kbuf.at[z, :, own_keys]
        return pltpu.make_async_remote_copy(
            src_ref=dst if half == 0 else kst, dst_ref=dst,
            send_sem=ks_s.at[t, half], recv_sem=ks_r.at[z, y],
            device_id=at(t, y if half == 0 else other), device_id_type=MESH)

    def key_wait(c, yy):
        pltpu.make_async_remote_copy(
            src_ref=kst, dst_ref=kbuf.at[c, :, pl.ds(aligned(yy * (T + PAD)), T + PAD)],
            send_sem=ks_s.at[z, 0], recv_sem=ks_r.at[c, yy],
            device_id=at(lax.rem(z + 1, Z), y), device_id_type=MESH).wait_recv()

    def key_send():
        if Y == 2:
            key_copy(z, 1).start()

        def one(i):
            for half in range(Y):
                key_copy(mate(i), half).start()

        loop(Z - 1, one)

    def key_recv(c):
        for yy in ([y] if Y == 1 else [y, other]):
            key_wait(c, yy)

    def key_drain(i):
        for half in range(Y):
            key_copy(mate(i), half).wait_send()

    v_sems = (vs_s, vs_r)

    own_off = off_ref[0].astype(F32)
    off_rows = jnp.full((PAD, D), own_off, F32).astype(BF16)
    loads[0].wait()
    tmp[0:T * G, :] = k_ref[...].astype(F32)
    for i in range(GL):
        kbuf[z, i, pl.ds(aligned(y * (T + PAD)), T), :] = head(tmp, G, first + i).astype(BF16)
        kbuf[z, i, pl.ds(aligned(y * (T + PAD) + T), PAD), :] = off_rows
        if Y == 2:
            kst[i, 0:T, :] = head(tmp, G, theirs + i).astype(BF16)
            kst[i, T:T + PAD, :] = off_rows
    pl.semaphore_wait(barrier, N - 1)
    key_send()

    def split_queries(dst, stage):
        for i in range(GL):
            for h in range(H):
                if Y == 2:
                    stage[i, pl.ds(h * T, T), :] = head(tmp, G * H, (theirs + i) * H + h).astype(BF16)
                dst[i, pl.ds(aligned(y * HT + h * T), T), :] = (
                    head(tmp, G * H, (first + i) * H + h).astype(BF16))


    loads[2].wait()
    tmp[0:T * G, :] = v_ref[...].astype(F32)
    for i in range(GL):
        vbuf[z, i, own_vals, :] = head(tmp, G, first + i).astype(BF16)
        if Y == 2:
            vst[i] = head(tmp, G, theirs + i).astype(BF16)
    y_start(1)
    loads[1].wait()
    tmp[...] = q_ref[...].astype(F32)
    split_queries(qs, qst)
    y_start(0)
    loads[3].wait()
    tmp[...] = do_ref[...].astype(F32)
    split_queries(dos, dost)
    y_wait(1)
    ag_send(vbuf, v_sems)
    y_start(2)

    loads[4].wait()
    tmp[...] = do_ref[...].astype(F32) * fo_ref[...].astype(F32)
    for i in range(GL):
        for h in range(H):
            def lanes(g):
                return jnp.sum(head(tmp, G * H, g * H + h).T, axis=0, keepdims=True)
            delta[i, :, pl.ds(pl.multiple_of(y * HT + h * T, 128), T)] = lanes(first + i)
            if Y == 2:
                delst[i, :, pl.ds(h * T, T)] = lanes(theirs + i)
    y_start(3)

    def key_rows(c, g):
        return jnp.concatenate([kbuf[c, g, pl.ds(i * (T + PAD), T), :] for i in range(Y)], axis=0)

    def block_off(c, i):
        return kbuf[c, 0, pl.ds(i * (T + PAD) + T, PAD), :][0:1, :].astype(F32)

    lead = (lax.broadcasted_iota(jnp.int32, (T, Q), 0)
            - lax.broadcasted_iota(jnp.int32, (T, Q), 1) % T).astype(F32)
    top_scr[...] = jnp.full(top_scr.shape, -1e30, F32)
    y_wait(0)
    if Y == 2:
        key_wait(z, other)
    q_off = jnp.concatenate([block_off(z, i) for i in range(Y) for h in range(H)], axis=1)

    def scores(c):
        for g in range(GL):
            s = dot_nt(key_rows(c, g), qs[g]) * (scale * LOG2E)
            parts = []
            for i in range(Y):
                off = jnp.concatenate([block_off(c, i)] * (Q // D), axis=1)
                parts.append(jnp.where(lead <= (q_off - off) * T, s[i * T:(i + 1) * T], -1e30))
            s = jnp.concatenate(parts, axis=0)
            s_scr[g, pl.ds(pl.multiple_of(c * C, 128), C), :] = s
            top_scr[g] = jnp.maximum(top_scr[g], jnp.max(s.reshape(C // 8, 8, Q), axis=0))

    scores(z)

    def key_arrival(i):
        key_recv(mate(i))
        scores(mate(i))

    loop(Z - 1, key_arrival)

    tops = [jnp.max(top_scr[g], axis=0, keepdims=True) for g in range(GL)]

    def total_step(c, sums):
        new = []
        for g in range(GL):
            rows = pl.ds(pl.multiple_of(c * C, 128), C)
            e = jnp.exp2(s_scr[g, rows, :] - tops[g])
            s_scr[g, rows, :] = e
            new.append(sums[g] + jnp.sum(e.reshape(C // 8, 8, Q), axis=0))
        return tuple(new)

    sums = lax.fori_loop(0, Z, total_step, tuple(jnp.zeros((8, Q), F32) for _ in range(GL)))
    inv = [1.0 / jnp.sum(t, axis=0, keepdims=True) for t in sums]

    y_wait(2)

    class Sums:
        def __init__(self, relayed, send, recv, own, mid, via, ss, rs, via_s, via_r):
            self.relayed = relayed and Z == 4
            self.send, self.recv, self.own, self.mid, self.via = send, recv, own, mid, via
            self.ss, self.rs, self.via_s, self.via_r = ss, rs, via_s, via_r

        def copy(self, c, half):
            return pltpu.make_async_remote_copy(
                src_ref=self.send.at[c, half], dst_ref=self.recv.at[z, y],
                send_sem=self.ss.at[c, half], recv_sem=self.rs.at[z, y],
                device_id=at(c, half), device_id_type=MESH)

        def arrive(self, src_z, src_y):
            pltpu.make_async_remote_copy(
                src_ref=self.send.at[z, y], dst_ref=self.recv.at[src_z, src_y],
                send_sem=self.ss.at[z, y], recv_sem=self.rs.at[src_z, src_y],
                device_id=at(lax.rem(z + 1, Z), y), device_id_type=MESH).wait_recv()

        def to_middle(self):
            return pltpu.make_async_remote_copy(
                src_ref=self.send.at[mate(Z - 2)], dst_ref=self.via,
                send_sem=self.via_s, recv_sem=self.via_r,
                device_id=at(mate(0), y), device_id_type=MESH)

        def start(self, c):
            for half in range(Y):
                self.copy(c, half).start()

    sum_v = Sums(True, gsv, grv, ownv, midv, viav, gv_s, gv_r, viav_s, viav_r)
    sum_k = Sums(False, gsk, grk, ownk, midk, viak, gk_s, gk_r, viak_s, viak_r)

    def value_chunk(c, put):
        rows = pl.ds(pl.multiple_of(c * C, 128), C)
        for g in range(GL):
            p = s_scr[g, rows, :] * inv[g]
            s_scr[g, rows, :] = p
            put(g, dot_nn(p.astype(BF16), dos[g]))

    def key_chunk(c, put):
        rows = pl.ds(pl.multiple_of(c * C, 128), C)
        for g in range(GL):
            dp = dot_nt(vbuf[c, g], dos[g])
            ds = (s_scr[g, rows, :] * (dp - delta[g])).astype(BF16)
            ds_scr[g, rows, :] = ds
            put(g, dot_nn(ds, qs[g]) * scale)

    def putter(ref):
        def put(g, x):
            for half in range(Y):
                ref[half, pl.ds(g * T, T), :] = x[half * T:(half + 1) * T].astype(ref.dtype)
        return put

    def send_chunks(chunk, sums):
        if not sums.relayed:
            def one(i):
                c = mate(i, False)
                chunk(c, putter(sums.send.at[c]))
                sums.start(c)
            loop(Z - 1, one)
            return

        @pl.when(jnp.logical_not(middle))
        def _():
            c = mate(2)
            chunk(c, putter(sums.send.at[c]))
            sums.to_middle().start()

        for i in (1, 0):
            c = mate(i)
            chunk(c, putter(sums.send.at[c]))
            sums.start(c)
        pl.when(middle)(lambda: chunk(mate(2), putter(sums.mid)))

    def own_chunk(chunk, sums):
        chunk(z, putter(sums.own))
        if Y == 2:
            sums.send[z, other] = sums.own[other].astype(BF16)
            sums.copy(z, other).start()

    def pass_on(sums):
        if sums.relayed:
            @pl.when(middle)
            def _():
                c = mate(2)
                sums.to_middle().wait_recv()
                sums.send[c] = (sums.mid[...] + sums.via[...].astype(F32)).astype(BF16)
                sums.start(c)

    send_chunks(value_chunk, sum_v)
    own_chunk(value_chunk, sum_v)
    y_wait(3)

    def key_arrival_grad(i):
        ag_recv(vbuf, i, v_sems)
        c = arrival(i)
        key_chunk(c, putter(sum_k.send.at[c]))
        sum_k.start(c)

    loop(Z - 1, key_arrival_grad)
    pass_on(sum_v)
    own_chunk(key_chunk, sum_k)

    for g in range(GL):
        kt = jnp.concatenate(
            [key_rows(c, g).astype(F32).T.astype(BF16) for c in range(Z)], axis=1)
        dqt = dot_nn(kt, ds_scr[g]) * scale
        for i in range(Y):
            for h in range(H):
                block = dqt[:, (i * H + h) * T:(i * H + h + 1) * T].T

                def keep(block=block, h=h):
                    dq_ref[pl.ds((first + g) * H + h, T, stride=G * H), :] = block

                def stage(block=block, h=h):
                    dqst[g, pl.ds(h * T, T), :] = block.astype(BF16)

                if Y == 2:
                    pl.when(y == i)(keep)
                    pl.when(y != i)(stage)
                else:
                    keep()
    y_start(4)

    def finish(out, sums):
        def add_from(src):
            sums.arrive(src, y)
            sums.own[y] = sums.own[y] + sums.recv[src, y].astype(F32)
            if Y == 2:
                sums.arrive(src, other)
                sums.own[other] = sums.own[other] + sums.recv[src, other].astype(F32)

        def add(i):
            if sums.relayed and i == 2:
                pl.when(middle)(lambda: add_from(mate(i)))
            else:
                add_from(mate(i))

        if Y == 2:
            sums.arrive(z, other)
            sums.own[other] = sums.recv[z, other].astype(F32)
        loop(Z - 1, add)
        for g in range(GL):
            out[pl.ds(first + g, T, stride=G), :] = sums.own[y, pl.ds(g * T, T), :]
            if Y == 2:
                out[pl.ds(theirs + g, T, stride=G), :] = sums.own[other, pl.ds(g * T, T), :]

    finish(dv_ref, sum_v)
    y_wait(4)
    if Y == 2:
        for g in range(GL):
            for h in range(H):
                dq_ref[pl.ds((theirs + g) * H + h, T, stride=G * H), :] = (
                    dqr[g, pl.ds(h * T, T), :].astype(F32))
    finish(dk_ref, sum_k)

    def drain(i):
        key_drain(i)
        ag_drain(vbuf, i, v_sems)
        for sums in (sum_v, sum_k):
            def direct(sums=sums):
                for half in range(Y):
                    sums.copy(mate(i), half).wait_send()

            if sums.relayed and i == 2:
                pl.when(middle)(direct)
                pl.when(jnp.logical_not(middle))(sums.to_middle().wait_send)
            else:
                direct()

    loop(Z - 1, drain)
    if Y == 2:
        key_copy(z, 1).wait_send()
        sum_v.copy(z, other).wait_send()
        sum_k.copy(z, other).wait_send()
    for cp in y_copies:
        cp.wait_send()


def hand_over(a_ref, b_ref, c_ref, a_out, b_out, c_out, a_mid, b_mid, c_mid, sem):
    ways = [(a_ref, a_mid, a_out), (b_ref, b_mid, b_out), (c_ref, c_mid, c_out)]
    ins = [pltpu.make_async_copy(w[0], w[1], sem.at[0, i]) for i, w in enumerate(ways)]
    outs = [pltpu.make_async_copy(w[1], w[2], sem.at[1, i]) for i, w in enumerate(ways)]
    for cp in ins:
        cp.start()
    for cp, out in zip(ins, outs):
        cp.wait()
        out.start()
    for out in outs:
        out.wait()


def on_device(Y, query_vectors, key_vectors, value_rows, forward_out, out_grad, block_offsets):
    T, QH, D = query_vectors.shape
    G = key_vectors.shape[1]
    H = QH // G
    N = lax.axis_size("ctx")
    Z = N // Y
    GL, C, HT, R = G // Y, Y * T, H * T, T * G
    Q = Y * HT
    vmem = pl.BlockSpec(memory_space=pltpu.VMEM)
    smem = pl.BlockSpec(memory_space=pltpu.SMEM)
    hbm = pl.BlockSpec(memory_space=pltpu.HBM)
    V = pltpu.VMEM
    own = V((Y, GL * T, D), F32)
    wire = V((Z, Y, GL * T, D), BF16)
    dq, dk, dv = pl.pallas_call(
        functools.partial(kernel, Z, Y, G, H, T, D),
        out_shape=(
            jax.ShapeDtypeStruct((T * QH, D), F32),
            jax.ShapeDtypeStruct((R, D), F32),
            jax.ShapeDtypeStruct((R, D), F32),
        ),
        in_specs=[hbm] * 5 + [smem],
        out_specs=[vmem] * 3,
        scratch_shapes=[
            V((T * QH, D), BF16), V((R, D), BF16), V((R, D), BF16),
            V((T * QH, D), BF16), V((T * QH, D), BF16), pltpu.SemaphoreType.DMA((5,)),
            V((T * QH, D), F32),
            V((GL, Q, D), BF16), V((GL, Q, D), BF16),
            V((GL, HT, D), BF16), V((GL, HT, D), BF16),
            V((GL, T + PAD, D), BF16), V((GL, T, D), BF16),
            V((GL, 1, Q), F32), V((GL, 1, HT), F32),
            V((Z, GL, Y * (T + PAD), D), BF16), V((Z, GL, C, D), BF16),
            V((GL, N * T, Q), F32), V((GL, N * T, Q), BF16), V((GL, 8, Q), F32),
            wire, wire, wire, wire, own, own, own, own, V((Y, GL * T, D), BF16), V((Y, GL * T, D), BF16),
            V((GL, HT, D), BF16), V((GL, HT, D), BF16),
            pltpu.SemaphoreType.DMA((5,)), pltpu.SemaphoreType.DMA((5,)),
        ] + [pltpu.SemaphoreType.DMA] * 4 + [pltpu.SemaphoreType.DMA((Z, Y))] * 2
        + [pltpu.SemaphoreType.DMA((Z,))] * 2 + [pltpu.SemaphoreType.DMA((Z, Y))] * 4,
        compiler_params=pltpu.CompilerParams(
            collective_id=0, has_side_effects=True, vmem_limit_bytes=56 * 1024 * 1024
        ),
        cost_estimate=pl.CostEstimate(
            flops=10 * GL * Q * N * T * D, bytes_accessed=4 * T * QH * D * 4,
            transcendentals=GL * Q * N * T,
        ),
    )(
        query_vectors.reshape(T * QH, D), key_vectors.reshape(R, D), value_rows.reshape(R, D),
        forward_out.reshape(T * QH, D), out_grad.reshape(T * QH, D), block_offsets,
    )
    dq, dk, dv = pl.pallas_call(
        hand_over,
        out_shape=[jax.ShapeDtypeStruct(x.shape, x.dtype) for x in (dq, dk, dv)],
        in_specs=[hbm] * 3,
        out_specs=[hbm] * 3,
        scratch_shapes=[V(x.shape, x.dtype) for x in (dq, dk, dv)] + [pltpu.SemaphoreType.DMA((2, 3))],
        compiler_params=pltpu.CompilerParams(vmem_limit_bytes=56 * 1024 * 1024),
        cost_estimate=pl.CostEstimate(
            flops=0, bytes_accessed=8 * (T * QH + 2 * R) * D, transcendentals=0),
    )(dq, dk, dv)
    return dq.reshape(T, QH, D), dk.reshape(T, G, D), dv.reshape(T, G, D)


def solution(mesh):
    pair = 2 if mesh.shape["groups"] == 2 and mesh.shape["ctx"] % 2 == 0 else 1
    tokens = P(("groups", "ctx"), "heads", None)
    return jax.shard_map(
        functools.partial(on_device, pair), mesh=mesh,
        in_specs=(tokens,) * 5 + (P(("groups", "ctx")),),
        out_specs=(tokens,) * 3, check_vma=False,
    )
```

```python
import functools

import jax
import jax.numpy as jnp
from jax import lax
from jax.experimental import pallas as pl
from jax.experimental.pallas import tpu as pltpu
from jax.sharding import PartitionSpec as P

MESH = pl.DeviceIdType.MESH
LOG2E = 1.4426950408889634
F32 = jnp.float32
BF16 = jnp.bfloat16
PAD = 16


def dot_nt(a, b):
    return lax.dot_general(a, b, (((1,), (1,)), ((), ())), preferred_element_type=F32)


def dot_nn(a, b):
    return lax.dot_general(a, b, (((1,), (0,)), ((), ())), preferred_element_type=F32)


def loop(n, body):
    if n <= 4:
        for i in range(n):
            body(i)
    else:
        def step(i, carry):
            body(i)
            return carry
        lax.fori_loop(0, n, step, 0)


def kernel(Z, Y, G, H, T, D, *refs):
    (q_hbm, k_hbm, v_hbm, fo_hbm, do_hbm, off_ref, dq_ref, dk_ref, dv_ref,
     q_ref, k_ref, v_ref, fo_ref, do_ref, in_sem,
     tmp, qs, dos, qst, dost, kst, vst, delta, delst, kbuf, vbuf,
     s_scr, ds_scr, top_scr,
     gsv, grv, gsk, grk, ownv, ownk, midv, midk, viav, viak,
     dqst, dqr, ys, yr, viav_s, viav_r, viak_s, viak_r,
     ks_s, ks_r, vs_s, vs_r, gv_s, gv_r, gk_s, gk_r) = refs
    me = lax.axis_index("ctx")
    z, y = me // Y, me % Y
    other = 1 - y if Y == 2 else 0
    scale = D ** (-0.5)
    GL = G // Y
    C = Y * T
    CP = Y * (T + PAD)
    HT = H * T
    N = Z * Y
    Q = Y * HT
    first = y * GL
    theirs = other * GL

    def at(zz, yy):
        return {"ctx": zz * Y + yy}

    inputs = [(k_hbm, k_ref), (q_hbm, q_ref), (v_hbm, v_ref), (do_hbm, do_ref), (fo_hbm, fo_ref)]
    loads = [pltpu.make_async_copy(a, b, in_sem.at[i]) for i, (a, b) in enumerate(inputs)]
    for cp in loads:
        cp.start()

    barrier = pltpu.get_barrier_semaphore()

    for d in range(Z):
        for yy in ([y] if d else []) + ([other] if Y == 2 else []):
            pl.semaphore_signal(
                barrier, inc=1, device_id=at(lax.rem(z + d, Z), yy), device_id_type=MESH)

    def head(src, heads, h):
        return tmp[pl.ds(h, T, stride=heads), :]

    def aligned(x):
        return pl.multiple_of(x, 16)

    def ycopy(i, src, dst):
        return pltpu.make_async_remote_copy(
            src_ref=src, dst_ref=dst, send_sem=ys.at[i], recv_sem=yr.at[i],
            device_id=at(z, other), device_id_type=MESH)

    own_rows = pl.ds(aligned(y * HT), HT)
    own_keys = pl.ds(aligned(y * (T + PAD)), T + PAD)
    own_vals = pl.ds(aligned(y * T), T)
    own_lanes = pl.ds(pl.multiple_of(y * HT, 128), HT)
    y_copies = []
    if Y == 2:
        y_copies = [
            ycopy(0, qst, qs.at[:, own_rows]),
            ycopy(1, vst, vbuf.at[z, :, own_vals]),
            ycopy(2, dost, dos.at[:, own_rows]),
            ycopy(3, delst, delta.at[:, :, own_lanes]),
            ycopy(4, dqst, dqr),
        ]

    def y_start(i):
        if Y == 2:
            y_copies[i].start()

    def y_wait(i):
        if Y == 2:
            y_copies[i].wait_recv()

    def mate(i, near=True):
        if not near:
            i = Z - 2 - i
        up = i + jnp.where(i >= z, 1, 0)
        v = Z - 1 - i
        return jnp.where(z < Z // 2, up, v - jnp.where(v <= z, 1, 0))

    def ag_copy(buf, t, block, sems):
        return pltpu.make_async_remote_copy(
            src_ref=buf.at[block], dst_ref=buf.at[block],
            send_sem=sems[0].at[t], recv_sem=sems[1].at[block],
            device_id=at(t, y), device_id_type=MESH)

    middle = (z > 0) & (z < Z - 1)

    relayed = Z == 4

    def ag_send(buf, sems):
        if not relayed:
            loop(Z - 1, lambda i: ag_copy(buf, mate(i), z, sems).start())
            return
        ag_copy(buf, mate(1), z, sems).start()
        ag_copy(buf, mate(0), z, sems).start()
        pl.when(middle)(lambda: ag_copy(buf, mate(2), z, sems).start())

    def ag_relay(buf, sems):
        return pltpu.make_async_remote_copy(
            src_ref=buf.at[mate(2)], dst_ref=buf.at[mate(2)],
            send_sem=sems[0].at[z], recv_sem=sems[1].at[mate(2)],
            device_id=at(Z - 1 - mate(2), y), device_id_type=MESH)

    def arrival(i):
        if not relayed or i == 0:
            return mate(i)
        return mate(jnp.where(middle, 3 - i, i))

    def ag_pass_on(buf, sems):
        if relayed:
            @pl.when(middle)
            def _():
                ag_copy(buf, mate(2), mate(2), sems).wait_recv()
                ag_relay(buf, sems).start()

    def ag_recv(buf, i, sems):
        copy = ag_copy(buf, arrival(i), arrival(i), sems)
        if relayed and i == 1:
            pl.when(jnp.logical_not(middle))(copy.wait_recv)
        else:
            copy.wait_recv()

    def ag_drain(buf, i, sems):
        if not relayed or i < 2:
            ag_copy(buf, mate(i), z, sems).wait_send()
            return
        pl.when(middle)(lambda: ag_copy(buf, mate(2), z, sems).wait_send())
        pl.when(middle)(lambda: ag_relay(buf, sems).wait_send())

    def key_copy(t, half):
        dst = kbuf.at[z, :, own_keys]
        return pltpu.make_async_remote_copy(
            src_ref=dst if half == 0 else kst, dst_ref=dst,
            send_sem=ks_s.at[t, half], recv_sem=ks_r.at[z, y],
            device_id=at(t, y if half == 0 else other), device_id_type=MESH)

    def key_wait(c, yy):
        pltpu.make_async_remote_copy(
            src_ref=kst, dst_ref=kbuf.at[c, :, pl.ds(aligned(yy * (T + PAD)), T + PAD)],
            send_sem=ks_s.at[z, 0], recv_sem=ks_r.at[c, yy],
            device_id=at(lax.rem(z + 1, Z), y), device_id_type=MESH).wait_recv()

    def key_send():
        if Y == 2:
            key_copy(z, 1).start()

        def one(i):
            for half in range(Y):
                key_copy(mate(i), half).start()

        loop(Z - 1, one)

    def key_recv(c):
        for yy in ([y] if Y == 1 else [y, other]):
            key_wait(c, yy)

    def key_drain(i):
        for half in range(Y):
            key_copy(mate(i), half).wait_send()

    v_sems = (vs_s, vs_r)

    own_off = off_ref[0].astype(F32)
    off_rows = jnp.full((PAD, D), own_off, F32).astype(BF16)
    loads[0].wait()
    tmp[0:T * G, :] = k_ref[...].astype(F32)
    for i in range(GL):
        kbuf[z, i, pl.ds(aligned(y * (T + PAD)), T), :] = head(tmp, G, first + i).astype(BF16)
        kbuf[z, i, pl.ds(aligned(y * (T + PAD) + T), PAD), :] = off_rows
        if Y == 2:
            kst[i, 0:T, :] = head(tmp, G, theirs + i).astype(BF16)
            kst[i, T:T + PAD, :] = off_rows
    pl.semaphore_wait(barrier, N - 1)
    key_send()

    def split_queries(dst, stage):
        for i in range(GL):
            for h in range(H):
                if Y == 2:
                    stage[i, pl.ds(h * T, T), :] = head(tmp, G * H, (theirs + i) * H + h).astype(BF16)
                dst[i, pl.ds(aligned(y * HT + h * T), T), :] = (
                    head(tmp, G * H, (first + i) * H + h).astype(BF16))


    loads[2].wait()
    tmp[0:T * G, :] = v_ref[...].astype(F32)
    for i in range(GL):
        vbuf[z, i, own_vals, :] = head(tmp, G, first + i).astype(BF16)
        if Y == 2:
            vst[i] = head(tmp, G, theirs + i).astype(BF16)
    y_start(1)
    loads[1].wait()
    tmp[...] = q_ref[...].astype(F32)
    split_queries(qs, qst)
    y_start(0)
    loads[3].wait()
    tmp[...] = do_ref[...].astype(F32)
    split_queries(dos, dost)
    y_wait(1)
    ag_send(vbuf, v_sems)
    y_start(2)

    loads[4].wait()
    tmp[...] = do_ref[...].astype(F32) * fo_ref[...].astype(F32)
    for i in range(GL):
        for h in range(H):
            def lanes(g):
                return jnp.sum(head(tmp, G * H, g * H + h).T, axis=0, keepdims=True)
            delta[i, :, pl.ds(pl.multiple_of(y * HT + h * T, 128), T)] = lanes(first + i)
            if Y == 2:
                delst[i, :, pl.ds(h * T, T)] = lanes(theirs + i)
    y_start(3)

    def key_rows(c, g):
        return jnp.concatenate([kbuf[c, g, pl.ds(i * (T + PAD), T), :] for i in range(Y)], axis=0)

    def block_off(c, i):
        return kbuf[c, 0, pl.ds(i * (T + PAD) + T, PAD), :][0:1, :].astype(F32)

    lead = (lax.broadcasted_iota(jnp.int32, (T, Q), 0)
            - lax.broadcasted_iota(jnp.int32, (T, Q), 1) % T).astype(F32)
    top_scr[...] = jnp.full(top_scr.shape, -1e30, F32)
    y_wait(0)
    if Y == 2:
        key_wait(z, other)
    q_off = jnp.concatenate([block_off(z, i) for i in range(Y) for h in range(H)], axis=1)

    def scores(c):
        for g in range(GL):
            s = dot_nt(key_rows(c, g), qs[g]) * (scale * LOG2E)
            parts = []
            for i in range(Y):
                off = jnp.concatenate([block_off(c, i)] * (Q // D), axis=1)
                parts.append(jnp.where(lead <= (q_off - off) * T, s[i * T:(i + 1) * T], -1e30))
            s = jnp.concatenate(parts, axis=0)
            s_scr[g, pl.ds(pl.multiple_of(c * C, 128), C), :] = s
            top_scr[g] = jnp.maximum(top_scr[g], jnp.max(s.reshape(C // 8, 8, Q), axis=0))

    scores(z)

    def key_arrival(i):
        key_recv(mate(i))
        scores(mate(i))

    loop(Z - 1, key_arrival)

    tops = [jnp.max(top_scr[g], axis=0, keepdims=True) for g in range(GL)]

    def total_step(c, sums):
        new = []
        for g in range(GL):
            rows = pl.ds(pl.multiple_of(c * C, 128), C)
            e = jnp.exp2(s_scr[g, rows, :] - tops[g])
            s_scr[g, rows, :] = e
            new.append(sums[g] + jnp.sum(e.reshape(C // 8, 8, Q), axis=0))
        return tuple(new)

    sums = lax.fori_loop(0, Z, total_step, tuple(jnp.zeros((8, Q), F32) for _ in range(GL)))
    ag_pass_on(vbuf, v_sems)
    inv = [1.0 / jnp.sum(t, axis=0, keepdims=True) for t in sums]

    y_wait(2)

    class Sums:
        def __init__(self, relayed, send, recv, own, mid, via, ss, rs, via_s, via_r):
            self.relayed = relayed and Z == 4
            self.send, self.recv, self.own, self.mid, self.via = send, recv, own, mid, via
            self.ss, self.rs, self.via_s, self.via_r = ss, rs, via_s, via_r

        def copy(self, c, half):
            return pltpu.make_async_remote_copy(
                src_ref=self.send.at[c, half], dst_ref=self.recv.at[z, y],
                send_sem=self.ss.at[c, half], recv_sem=self.rs.at[z, y],
                device_id=at(c, half), device_id_type=MESH)

        def arrive(self, src_z, src_y):
            pltpu.make_async_remote_copy(
                src_ref=self.send.at[z, y], dst_ref=self.recv.at[src_z, src_y],
                send_sem=self.ss.at[z, y], recv_sem=self.rs.at[src_z, src_y],
                device_id=at(lax.rem(z + 1, Z), y), device_id_type=MESH).wait_recv()

        def to_middle(self):
            return pltpu.make_async_remote_copy(
                src_ref=self.send.at[mate(Z - 2)], dst_ref=self.via,
                send_sem=self.via_s, recv_sem=self.via_r,
                device_id=at(mate(0), y), device_id_type=MESH)

        def start(self, c):
            for half in range(Y):
                self.copy(c, half).start()

    sum_v = Sums(True, gsv, grv, ownv, midv, viav, gv_s, gv_r, viav_s, viav_r)
    sum_k = Sums(False, gsk, grk, ownk, midk, viak, gk_s, gk_r, viak_s, viak_r)

    def value_chunk(c, put):
        rows = pl.ds(pl.multiple_of(c * C, 128), C)
        for g in range(GL):
            p = s_scr[g, rows, :] * inv[g]
            s_scr[g, rows, :] = p
            put(g, dot_nn(p.astype(BF16), dos[g]))

    def key_chunk(c, put):
        rows = pl.ds(pl.multiple_of(c * C, 128), C)
        for g in range(GL):
            dp = dot_nt(vbuf[c, g], dos[g])
            ds = (s_scr[g, rows, :] * (dp - delta[g])).astype(BF16)
            ds_scr[g, rows, :] = ds
            put(g, dot_nn(ds, qs[g]) * scale)

    def putter(ref):
        def put(g, x):
            for half in range(Y):
                ref[half, pl.ds(g * T, T), :] = x[half * T:(half + 1) * T].astype(ref.dtype)
        return put

    def send_chunks(chunk, sums):
        if not sums.relayed:
            def one(i):
                c = mate(i, False)
                chunk(c, putter(sums.send.at[c]))
                sums.start(c)
            loop(Z - 1, one)
            return

        @pl.when(jnp.logical_not(middle))
        def _():
            c = mate(2)
            chunk(c, putter(sums.send.at[c]))
            sums.to_middle().start()

        for i in (1, 0):
            c = mate(i)
            chunk(c, putter(sums.send.at[c]))
            sums.start(c)
        pl.when(middle)(lambda: chunk(mate(2), putter(sums.mid)))

    def own_chunk(chunk, sums):
        chunk(z, putter(sums.own))
        if Y == 2:
            sums.send[z, other] = sums.own[other].astype(BF16)
            sums.copy(z, other).start()

    def pass_on(sums):
        if sums.relayed:
            @pl.when(middle)
            def _():
                c = mate(2)
                sums.to_middle().wait_recv()
                sums.send[c] = (sums.mid[...] + sums.via[...].astype(F32)).astype(BF16)
                sums.start(c)

    send_chunks(value_chunk, sum_v)
    own_chunk(value_chunk, sum_v)
    y_wait(3)

    def key_arrival_grad(i):
        ag_recv(vbuf, i, v_sems)
        c = arrival(i)
        key_chunk(c, putter(sum_k.send.at[c]))
        sum_k.start(c)

    loop(Z - 1, key_arrival_grad)
    pass_on(sum_v)
    own_chunk(key_chunk, sum_k)

    for g in range(GL):
        kt = jnp.concatenate(
            [key_rows(c, g).astype(F32).T.astype(BF16) for c in range(Z)], axis=1)
        dqt = dot_nn(kt, ds_scr[g]) * scale
        for i in range(Y):
            for h in range(H):
                block = dqt[:, (i * H + h) * T:(i * H + h + 1) * T].T

                def keep(block=block, h=h):
                    dq_ref[pl.ds((first + g) * H + h, T, stride=G * H), :] = block

                def stage(block=block, h=h):
                    dqst[g, pl.ds(h * T, T), :] = block.astype(BF16)

                if Y == 2:
                    pl.when(y == i)(keep)
                    pl.when(y != i)(stage)
                else:
                    keep()
    y_start(4)

    def finish(out, sums):
        def add_from(src):
            sums.arrive(src, y)
            sums.own[y] = sums.own[y] + sums.recv[src, y].astype(F32)
            if Y == 2:
                sums.arrive(src, other)
                sums.own[other] = sums.own[other] + sums.recv[src, other].astype(F32)

        def add(i):
            if sums.relayed and i == 2:
                pl.when(middle)(lambda: add_from(mate(i)))
            else:
                add_from(mate(i))

        if Y == 2:
            sums.arrive(z, other)
            sums.own[other] = sums.recv[z, other].astype(F32)
        loop(Z - 1, add)
        for g in range(GL):
            out[pl.ds(first + g, T, stride=G), :] = sums.own[y, pl.ds(g * T, T), :]
            if Y == 2:
                out[pl.ds(theirs + g, T, stride=G), :] = sums.own[other, pl.ds(g * T, T), :]

    finish(dv_ref, sum_v)
    y_wait(4)
    if Y == 2:
        for g in range(GL):
            for h in range(H):
                dq_ref[pl.ds((theirs + g) * H + h, T, stride=G * H), :] = (
                    dqr[g, pl.ds(h * T, T), :].astype(F32))
    finish(dk_ref, sum_k)

    def drain(i):
        key_drain(i)
        ag_drain(vbuf, i, v_sems)
        for sums in (sum_v, sum_k):
            def direct(sums=sums):
                for half in range(Y):
                    sums.copy(mate(i), half).wait_send()

            if sums.relayed and i == 2:
                pl.when(middle)(direct)
                pl.when(jnp.logical_not(middle))(sums.to_middle().wait_send)
            else:
                direct()

    loop(Z - 1, drain)
    if Y == 2:
        key_copy(z, 1).wait_send()
        sum_v.copy(z, other).wait_send()
        sum_k.copy(z, other).wait_send()
    for cp in y_copies:
        cp.wait_send()


def hand_over(a_ref, b_ref, c_ref, a_out, b_out, c_out, a_mid, b_mid, c_mid, sem):
    ways = [(a_ref, a_mid, a_out), (b_ref, b_mid, b_out), (c_ref, c_mid, c_out)]
    ins = [pltpu.make_async_copy(w[0], w[1], sem.at[0, i]) for i, w in enumerate(ways)]
    outs = [pltpu.make_async_copy(w[1], w[2], sem.at[1, i]) for i, w in enumerate(ways)]
    for cp in ins:
        cp.start()
    for cp, out in zip(ins, outs):
        cp.wait()
        out.start()
    for out in outs:
        out.wait()


def on_device(Y, query_vectors, key_vectors, value_rows, forward_out, out_grad, block_offsets):
    T, QH, D = query_vectors.shape
    G = key_vectors.shape[1]
    H = QH // G
    N = lax.axis_size("ctx")
    Z = N // Y
    GL, C, HT, R = G // Y, Y * T, H * T, T * G
    Q = Y * HT
    vmem = pl.BlockSpec(memory_space=pltpu.VMEM)
    smem = pl.BlockSpec(memory_space=pltpu.SMEM)
    hbm = pl.BlockSpec(memory_space=pltpu.HBM)
    V = pltpu.VMEM
    own = V((Y, GL * T, D), F32)
    wire = V((Z, Y, GL * T, D), BF16)
    dq, dk, dv = pl.pallas_call(
        functools.partial(kernel, Z, Y, G, H, T, D),
        out_shape=(
            jax.ShapeDtypeStruct((T * QH, D), F32),
            jax.ShapeDtypeStruct((R, D), F32),
            jax.ShapeDtypeStruct((R, D), F32),
        ),
        in_specs=[hbm] * 5 + [smem],
        out_specs=[vmem] * 3,
        scratch_shapes=[
            V((T * QH, D), BF16), V((R, D), BF16), V((R, D), BF16),
            V((T * QH, D), BF16), V((T * QH, D), BF16), pltpu.SemaphoreType.DMA((5,)),
            V((T * QH, D), F32),
            V((GL, Q, D), BF16), V((GL, Q, D), BF16),
            V((GL, HT, D), BF16), V((GL, HT, D), BF16),
            V((GL, T + PAD, D), BF16), V((GL, T, D), BF16),
            V((GL, 1, Q), F32), V((GL, 1, HT), F32),
            V((Z, GL, Y * (T + PAD), D), BF16), V((Z, GL, C, D), BF16),
            V((GL, N * T, Q), F32), V((GL, N * T, Q), BF16), V((GL, 8, Q), F32),
            wire, wire, wire, wire, own, own, own, own, V((Y, GL * T, D), BF16), V((Y, GL * T, D), BF16),
            V((GL, HT, D), BF16), V((GL, HT, D), BF16),
            pltpu.SemaphoreType.DMA((5,)), pltpu.SemaphoreType.DMA((5,)),
        ] + [pltpu.SemaphoreType.DMA] * 4 + [pltpu.SemaphoreType.DMA((Z, Y))] * 2
        + [pltpu.SemaphoreType.DMA((Z,))] * 2 + [pltpu.SemaphoreType.DMA((Z, Y))] * 4,
        compiler_params=pltpu.CompilerParams(
            collective_id=0, has_side_effects=True, vmem_limit_bytes=56 * 1024 * 1024
        ),
        cost_estimate=pl.CostEstimate(
            flops=10 * GL * Q * N * T * D, bytes_accessed=4 * T * QH * D * 4,
            transcendentals=GL * Q * N * T,
        ),
    )(
        query_vectors.reshape(T * QH, D), key_vectors.reshape(R, D), value_rows.reshape(R, D),
        forward_out.reshape(T * QH, D), out_grad.reshape(T * QH, D), block_offsets,
    )
    dq, dk, dv = pl.pallas_call(
        hand_over,
        out_shape=[jax.ShapeDtypeStruct(x.shape, x.dtype) for x in (dq, dk, dv)],
        in_specs=[hbm] * 3,
        out_specs=[hbm] * 3,
        scratch_shapes=[V(x.shape, x.dtype) for x in (dq, dk, dv)] + [pltpu.SemaphoreType.DMA((2, 3))],
        compiler_params=pltpu.CompilerParams(vmem_limit_bytes=56 * 1024 * 1024),
        cost_estimate=pl.CostEstimate(
            flops=0, bytes_accessed=8 * (T * QH + 2 * R) * D, transcendentals=0),
    )(dq, dk, dv)
    return dq.reshape(T, QH, D), dk.reshape(T, G, D), dv.reshape(T, G, D)


def solution(mesh):
    pair = 2 if mesh.shape["groups"] == 2 and mesh.shape["ctx"] % 2 == 0 else 1
    tokens = P(("groups", "ctx"), "heads", None)
    return jax.shard_map(
        functools.partial(on_device, pair), mesh=mesh,
        in_specs=(tokens,) * 5 + (P(("groups", "ctx")),),
        out_specs=(tokens,) * 3, check_vma=False,
    )
```

```python
import functools

import jax
import jax.numpy as jnp
from jax import lax
from jax.experimental import pallas as pl
from jax.experimental.pallas import tpu as pltpu
from jax.sharding import PartitionSpec as P

MESH = pl.DeviceIdType.MESH
LOG2E = 1.4426950408889634
F32 = jnp.float32
BF16 = jnp.bfloat16
PAD = 16


def dot_nt(a, b):
    return lax.dot_general(a, b, (((1,), (1,)), ((), ())), preferred_element_type=F32)


def dot_nn(a, b):
    return lax.dot_general(a, b, (((1,), (0,)), ((), ())), preferred_element_type=F32)


def loop(n, body):
    if n <= 4:
        for i in range(n):
            body(i)
    else:
        def step(i, carry):
            body(i)
            return carry
        lax.fori_loop(0, n, step, 0)


def kernel(Z, Y, G, H, T, D, *refs):
    (q_hbm, k_hbm, v_hbm, fo_hbm, do_hbm, off_ref, dq_ref, dk_ref, dv_ref,
     q_ref, k_ref, v_ref, fo_ref, do_ref, in_sem,
     tmp, qs, dos, qst, dost, kst, vst, delta, delst, kbuf, vbuf,
     s_scr, ds_scr, top_scr,
     gsv, grv, gsk, grk, ownv, ownk, midv, midk, viav, viak,
     dqst, dqr, ys, yr, viav_s, viav_r, viak_s, viak_r,
     ks_s, ks_r, vs_s, vs_r, gv_s, gv_r, gk_s, gk_r) = refs
    me = lax.axis_index("ctx")
    z, y = me // Y, me % Y
    other = 1 - y if Y == 2 else 0
    scale = D ** (-0.5)
    GL = G // Y
    C = Y * T
    CP = Y * (T + PAD)
    HT = H * T
    N = Z * Y
    Q = Y * HT
    first = y * GL
    theirs = other * GL

    def at(zz, yy):
        return {"ctx": zz * Y + yy}

    inputs = [(k_hbm, k_ref), (q_hbm, q_ref), (v_hbm, v_ref), (do_hbm, do_ref), (fo_hbm, fo_ref)]
    loads = [pltpu.make_async_copy(a, b, in_sem.at[i]) for i, (a, b) in enumerate(inputs)]
    for cp in loads:
        cp.start()

    barrier = pltpu.get_barrier_semaphore()

    for d in range(Z):
        for yy in ([y] if d else []) + ([other] if Y == 2 else []):
            pl.semaphore_signal(
                barrier, inc=1, device_id=at(lax.rem(z + d, Z), yy), device_id_type=MESH)

    def head(src, heads, h):
        return tmp[pl.ds(h, T, stride=heads), :]

    def aligned(x):
        return pl.multiple_of(x, 16)

    def ycopy(i, src, dst):
        return pltpu.make_async_remote_copy(
            src_ref=src, dst_ref=dst, send_sem=ys.at[i], recv_sem=yr.at[i],
            device_id=at(z, other), device_id_type=MESH)

    own_rows = pl.ds(aligned(y * HT), HT)
    own_keys = pl.ds(aligned(y * (T + PAD)), T + PAD)
    own_vals = pl.ds(aligned(y * T), T)
    own_lanes = pl.ds(pl.multiple_of(y * HT, 128), HT)
    y_copies = []
    if Y == 2:
        y_copies = [
            ycopy(0, qst, qs.at[:, own_rows]),
            ycopy(1, vst, vbuf.at[z, :, own_vals]),
            ycopy(2, dost, dos.at[:, own_rows]),
            ycopy(3, delst, delta.at[:, :, own_lanes]),
            ycopy(4, dqst, dqr),
        ]

    def y_start(i):
        if Y == 2:
            y_copies[i].start()

    def y_wait(i):
        if Y == 2:
            y_copies[i].wait_recv()

    def mate(i, near=True):
        if not near:
            i = Z - 2 - i
        up = i + jnp.where(i >= z, 1, 0)
        v = Z - 1 - i
        return jnp.where(z < Z // 2, up, v - jnp.where(v <= z, 1, 0))

    def ag_copy(buf, t, block, sems):
        return pltpu.make_async_remote_copy(
            src_ref=buf.at[block], dst_ref=buf.at[block],
            send_sem=sems[0].at[t], recv_sem=sems[1].at[block],
            device_id=at(t, y), device_id_type=MESH)

    middle = (z > 0) & (z < Z - 1)

    relayed = Z == 4

    def ag_send(buf, sems):
        if not relayed:
            loop(Z - 1, lambda i: ag_copy(buf, mate(i), z, sems).start())
            return
        ag_copy(buf, mate(1), z, sems).start()
        ag_copy(buf, mate(0), z, sems).start()
        pl.when(middle)(lambda: ag_copy(buf, mate(2), z, sems).start())

    def ag_relay(buf, sems):
        return pltpu.make_async_remote_copy(
            src_ref=buf.at[mate(2)], dst_ref=buf.at[mate(2)],
            send_sem=sems[0].at[z], recv_sem=sems[1].at[mate(2)],
            device_id=at(Z - 1 - mate(2), y), device_id_type=MESH)

    def arrival(i):
        if not relayed or i == 0:
            return mate(i)
        return mate(jnp.where(middle, 3 - i, i))

    def ag_pass_on(buf, sems):
        if relayed:
            @pl.when(middle)
            def _():
                ag_copy(buf, mate(2), mate(2), sems).wait_recv()
                ag_relay(buf, sems).start()

    def ag_recv(buf, i, sems):
        copy = ag_copy(buf, arrival(i), arrival(i), sems)
        if relayed and i == 1:
            pl.when(jnp.logical_not(middle))(copy.wait_recv)
        else:
            copy.wait_recv()

    def ag_drain(buf, i, sems):
        if not relayed or i < 2:
            ag_copy(buf, mate(i), z, sems).wait_send()
            return
        pl.when(middle)(lambda: ag_copy(buf, mate(2), z, sems).wait_send())
        pl.when(middle)(lambda: ag_relay(buf, sems).wait_send())

    def key_copy(t, half):
        dst = kbuf.at[z, :, own_keys]
        return pltpu.make_async_remote_copy(
            src_ref=dst if half == 0 else kst, dst_ref=dst,
            send_sem=ks_s.at[t, half], recv_sem=ks_r.at[z, y],
            device_id=at(t, y if half == 0 else other), device_id_type=MESH)

    def key_wait(c, yy):
        pltpu.make_async_remote_copy(
            src_ref=kst, dst_ref=kbuf.at[c, :, pl.ds(aligned(yy * (T + PAD)), T + PAD)],
            send_sem=ks_s.at[z, 0], recv_sem=ks_r.at[c, yy],
            device_id=at(lax.rem(z + 1, Z), y), device_id_type=MESH).wait_recv()

    def key_send():
        if Y == 2:
            key_copy(z, 1).start()

        def one(i):
            for half in range(Y):
                key_copy(mate(i), half).start()

        loop(Z - 1, one)

    def key_recv(c):
        for yy in ([y] if Y == 1 else [y, other]):
            key_wait(c, yy)

    def key_drain(i):
        for half in range(Y):
            key_copy(mate(i), half).wait_send()

    v_sems = (vs_s, vs_r)

    own_off = off_ref[0].astype(F32)
    off_rows = jnp.full((PAD, D), own_off, F32).astype(BF16)
    loads[0].wait()
    tmp[0:T * G, :] = k_ref[...].astype(F32)
    for i in range(GL):
        kbuf[z, i, pl.ds(aligned(y * (T + PAD)), T), :] = head(tmp, G, first + i).astype(BF16)
        kbuf[z, i, pl.ds(aligned(y * (T + PAD) + T), PAD), :] = off_rows
        if Y == 2:
            kst[i, 0:T, :] = head(tmp, G, theirs + i).astype(BF16)
            kst[i, T:T + PAD, :] = off_rows
    pl.semaphore_wait(barrier, N - 1)
    key_send()

    def split_queries(dst, stage):
        for i in range(GL):
            for h in range(H):
                if Y == 2:
                    stage[i, pl.ds(h * T, T), :] = head(tmp, G * H, (theirs + i) * H + h).astype(BF16)
                dst[i, pl.ds(aligned(y * HT + h * T), T), :] = (
                    head(tmp, G * H, (first + i) * H + h).astype(BF16))


    loads[2].wait()
    tmp[0:T * G, :] = v_ref[...].astype(F32)
    for i in range(GL):
        vbuf[z, i, own_vals, :] = head(tmp, G, first + i).astype(BF16)
        if Y == 2:
            vst[i] = head(tmp, G, theirs + i).astype(BF16)
    y_start(1)
    loads[1].wait()
    tmp[...] = q_ref[...].astype(F32)
    split_queries(qs, qst)
    y_start(0)
    loads[3].wait()
    tmp[...] = do_ref[...].astype(F32)
    split_queries(dos, dost)
    y_wait(1)
    ag_send(vbuf, v_sems)
    y_start(2)

    loads[4].wait()
    tmp[...] = do_ref[...].astype(F32) * fo_ref[...].astype(F32)
    for i in range(GL):
        for h in range(H):
            def lanes(g):
                return jnp.sum(head(tmp, G * H, g * H + h).T, axis=0, keepdims=True)
            delta[i, :, pl.ds(pl.multiple_of(y * HT + h * T, 128), T)] = lanes(first + i)
            if Y == 2:
                delst[i, :, pl.ds(h * T, T)] = lanes(theirs + i)
    y_start(3)

    def key_rows(c, g):
        return jnp.concatenate([kbuf[c, g, pl.ds(i * (T + PAD), T), :] for i in range(Y)], axis=0)

    def block_off(c, i):
        return kbuf[c, 0, pl.ds(i * (T + PAD) + T, PAD), :][0:1, :].astype(F32)

    lead = (lax.broadcasted_iota(jnp.int32, (T, Q), 0)
            - lax.broadcasted_iota(jnp.int32, (T, Q), 1) % T).astype(F32)
    top_scr[...] = jnp.full(top_scr.shape, -1e30, F32)
    y_wait(0)
    if Y == 2:
        key_wait(z, other)
    q_off = jnp.concatenate([block_off(z, i) for i in range(Y) for h in range(H)], axis=1)

    def scores(c):
        for g in range(GL):
            s = dot_nt(key_rows(c, g), qs[g]) * (scale * LOG2E)
            parts = []
            for i in range(Y):
                off = jnp.concatenate([block_off(c, i)] * (Q // D), axis=1)
                parts.append(jnp.where(lead <= (q_off - off) * T, s[i * T:(i + 1) * T], -1e30))
            s = jnp.concatenate(parts, axis=0)
            s_scr[g, pl.ds(pl.multiple_of(c * C, 128), C), :] = s
            top_scr[g] = jnp.maximum(top_scr[g], jnp.max(s.reshape(C // 8, 8, Q), axis=0))

    scores(z)

    def key_arrival(i):
        key_recv(mate(i))
        scores(mate(i))

    loop(Z - 1, key_arrival)

    tops = [jnp.max(top_scr[g], axis=0, keepdims=True) for g in range(GL)]

    def total_step(c, sums):
        new = []
        for g in range(GL):
            rows = pl.ds(pl.multiple_of(c * C, 128), C)
            e = jnp.exp2(s_scr[g, rows, :] - tops[g])
            s_scr[g, rows, :] = e
            new.append(sums[g] + jnp.sum(e.reshape(C // 8, 8, Q), axis=0))
        return tuple(new)

    ag_pass_on(vbuf, v_sems)
    sums = lax.fori_loop(0, Z, total_step, tuple(jnp.zeros((8, Q), F32) for _ in range(GL)))
    inv = [1.0 / jnp.sum(t, axis=0, keepdims=True) for t in sums]

    y_wait(2)

    class Sums:
        def __init__(self, relayed, send, recv, own, mid, via, ss, rs, via_s, via_r):
            self.relayed = relayed and Z == 4
            self.send, self.recv, self.own, self.mid, self.via = send, recv, own, mid, via
            self.ss, self.rs, self.via_s, self.via_r = ss, rs, via_s, via_r

        def copy(self, c, half):
            return pltpu.make_async_remote_copy(
                src_ref=self.send.at[c, half], dst_ref=self.recv.at[z, y],
                send_sem=self.ss.at[c, half], recv_sem=self.rs.at[z, y],
                device_id=at(c, half), device_id_type=MESH)

        def arrive(self, src_z, src_y):
            pltpu.make_async_remote_copy(
                src_ref=self.send.at[z, y], dst_ref=self.recv.at[src_z, src_y],
                send_sem=self.ss.at[z, y], recv_sem=self.rs.at[src_z, src_y],
                device_id=at(lax.rem(z + 1, Z), y), device_id_type=MESH).wait_recv()

        def to_middle(self):
            return pltpu.make_async_remote_copy(
                src_ref=self.send.at[mate(Z - 2)], dst_ref=self.via,
                send_sem=self.via_s, recv_sem=self.via_r,
                device_id=at(mate(0), y), device_id_type=MESH)

        def start(self, c):
            for half in range(Y):
                self.copy(c, half).start()

    sum_v = Sums(True, gsv, grv, ownv, midv, viav, gv_s, gv_r, viav_s, viav_r)
    sum_k = Sums(False, gsk, grk, ownk, midk, viak, gk_s, gk_r, viak_s, viak_r)

    def value_chunk(c, put):
        rows = pl.ds(pl.multiple_of(c * C, 128), C)
        for g in range(GL):
            p = s_scr[g, rows, :] * inv[g]
            s_scr[g, rows, :] = p
            put(g, dot_nn(p.astype(BF16), dos[g]))

    def key_chunk(c, put):
        rows = pl.ds(pl.multiple_of(c * C, 128), C)
        for g in range(GL):
            dp = dot_nt(vbuf[c, g], dos[g])
            ds = (s_scr[g, rows, :] * (dp - delta[g])).astype(BF16)
            ds_scr[g, rows, :] = ds
            put(g, dot_nn(ds, qs[g]) * scale)

    def putter(ref):
        def put(g, x):
            for half in range(Y):
                ref[half, pl.ds(g * T, T), :] = x[half * T:(half + 1) * T].astype(ref.dtype)
        return put

    def send_chunks(chunk, sums):
        if not sums.relayed:
            def one(i):
                c = mate(i, False)
                chunk(c, putter(sums.send.at[c]))
                sums.start(c)
            loop(Z - 1, one)
            return

        @pl.when(jnp.logical_not(middle))
        def _():
            c = mate(2)
            chunk(c, putter(sums.send.at[c]))
            sums.to_middle().start()

        for i in (1, 0):
            c = mate(i)
            chunk(c, putter(sums.send.at[c]))
            sums.start(c)
        pl.when(middle)(lambda: chunk(mate(2), putter(sums.mid)))

    def own_chunk(chunk, sums):
        chunk(z, putter(sums.own))
        if Y == 2:
            sums.send[z, other] = sums.own[other].astype(BF16)
            sums.copy(z, other).start()

    def pass_on(sums):
        if sums.relayed:
            @pl.when(middle)
            def _():
                c = mate(2)
                sums.to_middle().wait_recv()
                sums.send[c] = (sums.mid[...] + sums.via[...].astype(F32)).astype(BF16)
                sums.start(c)

    send_chunks(value_chunk, sum_v)
    own_chunk(value_chunk, sum_v)
    y_wait(3)

    def key_arrival_grad(i):
        ag_recv(vbuf, i, v_sems)
        c = arrival(i)
        key_chunk(c, putter(sum_k.send.at[c]))
        sum_k.start(c)

    loop(Z - 1, key_arrival_grad)
    pass_on(sum_v)
    own_chunk(key_chunk, sum_k)

    for g in range(GL):
        kt = jnp.concatenate(
            [key_rows(c, g).astype(F32).T.astype(BF16) for c in range(Z)], axis=1)
        dqt = dot_nn(kt, ds_scr[g]) * scale
        for i in range(Y):
            for h in range(H):
                block = dqt[:, (i * H + h) * T:(i * H + h + 1) * T].T

                def keep(block=block, h=h):
                    dq_ref[pl.ds((first + g) * H + h, T, stride=G * H), :] = block

                def stage(block=block, h=h):
                    dqst[g, pl.ds(h * T, T), :] = block.astype(BF16)

                if Y == 2:
                    pl.when(y == i)(keep)
                    pl.when(y != i)(stage)
                else:
                    keep()
    y_start(4)

    def finish(out, sums):
        def add_from(src):
            sums.arrive(src, y)
            sums.own[y] = sums.own[y] + sums.recv[src, y].astype(F32)
            if Y == 2:
                sums.arrive(src, other)
                sums.own[other] = sums.own[other] + sums.recv[src, other].astype(F32)

        def add(i):
            if sums.relayed and i == 2:
                pl.when(middle)(lambda: add_from(mate(i)))
            else:
                add_from(mate(i))

        if Y == 2:
            sums.arrive(z, other)
            sums.own[other] = sums.recv[z, other].astype(F32)
        loop(Z - 1, add)
        for g in range(GL):
            out[pl.ds(first + g, T, stride=G), :] = sums.own[y, pl.ds(g * T, T), :]
            if Y == 2:
                out[pl.ds(theirs + g, T, stride=G), :] = sums.own[other, pl.ds(g * T, T), :]

    finish(dv_ref, sum_v)
    y_wait(4)
    if Y == 2:
        for g in range(GL):
            for h in range(H):
                dq_ref[pl.ds((theirs + g) * H + h, T, stride=G * H), :] = (
                    dqr[g, pl.ds(h * T, T), :].astype(F32))
    finish(dk_ref, sum_k)

    def drain(i):
        key_drain(i)
        ag_drain(vbuf, i, v_sems)
        for sums in (sum_v, sum_k):
            def direct(sums=sums):
                for half in range(Y):
                    sums.copy(mate(i), half).wait_send()

            if sums.relayed and i == 2:
                pl.when(middle)(direct)
                pl.when(jnp.logical_not(middle))(sums.to_middle().wait_send)
            else:
                direct()

    loop(Z - 1, drain)
    if Y == 2:
        key_copy(z, 1).wait_send()
        sum_v.copy(z, other).wait_send()
        sum_k.copy(z, other).wait_send()
    for cp in y_copies:
        cp.wait_send()


def hand_over(a_ref, b_ref, c_ref, a_out, b_out, c_out, a_mid, b_mid, c_mid, sem):
    ways = [(a_ref, a_mid, a_out), (b_ref, b_mid, b_out), (c_ref, c_mid, c_out)]
    ins = [pltpu.make_async_copy(w[0], w[1], sem.at[0, i]) for i, w in enumerate(ways)]
    outs = [pltpu.make_async_copy(w[1], w[2], sem.at[1, i]) for i, w in enumerate(ways)]
    for cp in ins:
        cp.start()
    for cp, out in zip(ins, outs):
        cp.wait()
        out.start()
    for out in outs:
        out.wait()


def on_device(Y, query_vectors, key_vectors, value_rows, forward_out, out_grad, block_offsets):
    T, QH, D = query_vectors.shape
    G = key_vectors.shape[1]
    H = QH // G
    N = lax.axis_size("ctx")
    Z = N // Y
    GL, C, HT, R = G // Y, Y * T, H * T, T * G
    Q = Y * HT
    vmem = pl.BlockSpec(memory_space=pltpu.VMEM)
    smem = pl.BlockSpec(memory_space=pltpu.SMEM)
    hbm = pl.BlockSpec(memory_space=pltpu.HBM)
    V = pltpu.VMEM
    own = V((Y, GL * T, D), F32)
    wire = V((Z, Y, GL * T, D), BF16)
    dq, dk, dv = pl.pallas_call(
        functools.partial(kernel, Z, Y, G, H, T, D),
        out_shape=(
            jax.ShapeDtypeStruct((T * QH, D), F32),
            jax.ShapeDtypeStruct((R, D), F32),
            jax.ShapeDtypeStruct((R, D), F32),
        ),
        in_specs=[hbm] * 5 + [smem],
        out_specs=[vmem] * 3,
        scratch_shapes=[
            V((T * QH, D), BF16), V((R, D), BF16), V((R, D), BF16),
            V((T * QH, D), BF16), V((T * QH, D), BF16), pltpu.SemaphoreType.DMA((5,)),
            V((T * QH, D), F32),
            V((GL, Q, D), BF16), V((GL, Q, D), BF16),
            V((GL, HT, D), BF16), V((GL, HT, D), BF16),
            V((GL, T + PAD, D), BF16), V((GL, T, D), BF16),
            V((GL, 1, Q), F32), V((GL, 1, HT), F32),
            V((Z, GL, Y * (T + PAD), D), BF16), V((Z, GL, C, D), BF16),
            V((GL, N * T, Q), F32), V((GL, N * T, Q), BF16), V((GL, 8, Q), F32),
            wire, wire, wire, wire, own, own, own, own, V((Y, GL * T, D), BF16), V((Y, GL * T, D), BF16),
            V((GL, HT, D), BF16), V((GL, HT, D), BF16),
            pltpu.SemaphoreType.DMA((5,)), pltpu.SemaphoreType.DMA((5,)),
        ] + [pltpu.SemaphoreType.DMA] * 4 + [pltpu.SemaphoreType.DMA((Z, Y))] * 2
        + [pltpu.SemaphoreType.DMA((Z,))] * 2 + [pltpu.SemaphoreType.DMA((Z, Y))] * 4,
        compiler_params=pltpu.CompilerParams(
            collective_id=0, has_side_effects=True, vmem_limit_bytes=56 * 1024 * 1024
        ),
        cost_estimate=pl.CostEstimate(
            flops=10 * GL * Q * N * T * D, bytes_accessed=4 * T * QH * D * 4,
            transcendentals=GL * Q * N * T,
        ),
    )(
        query_vectors.reshape(T * QH, D), key_vectors.reshape(R, D), value_rows.reshape(R, D),
        forward_out.reshape(T * QH, D), out_grad.reshape(T * QH, D), block_offsets,
    )
    dq, dk, dv = pl.pallas_call(
        hand_over,
        out_shape=[jax.ShapeDtypeStruct(x.shape, x.dtype) for x in (dq, dk, dv)],
        in_specs=[hbm] * 3,
        out_specs=[hbm] * 3,
        scratch_shapes=[V(x.shape, x.dtype) for x in (dq, dk, dv)] + [pltpu.SemaphoreType.DMA((2, 3))],
        compiler_params=pltpu.CompilerParams(vmem_limit_bytes=56 * 1024 * 1024),
        cost_estimate=pl.CostEstimate(
            flops=0, bytes_accessed=8 * (T * QH + 2 * R) * D, transcendentals=0),
    )(dq, dk, dv)
    return dq.reshape(T, QH, D), dk.reshape(T, G, D), dv.reshape(T, G, D)


def solution(mesh):
    pair = 2 if mesh.shape["groups"] == 2 and mesh.shape["ctx"] % 2 == 0 else 1
    tokens = P(("groups", "ctx"), "heads", None)
    return jax.shard_map(
        functools.partial(on_device, pair), mesh=mesh,
        in_specs=(tokens,) * 5 + (P(("groups", "ctx")),),
        out_specs=(tokens,) * 3, check_vma=False,
    )
```
